256 devices in a mesh: row: 16 (over z_lo, x, core), col: 16 (over y, z_hi).
Axes of the slice: x: 4, y: 4, z: 8 (z_hi: 4, z_lo: 2; z = z_hi * 2 + z_lo), core: 2. Of those that a mesh axis runs over, the one named last changes fastest.
Arguments:
- embed_docs: float32 [16384, 256], P(('row', 'col')), may hold values from -2 to 2
- embed_targets: float32 [32768, 256], P(('col', 'row')), may hold values from -2 to 2
- starting_goal_multiplier: float32 [32768], P('col'), may hold values from -0.8 to 0.8
Outputs:
- grad_docs: float32 [16384, 256], P(('row', 'col'))
- grad_targets: float32 [32768, 256], P(('col', 'row'))
The draws below stay inside these ranges and needn't reach their ends.
All inputs are finite; a program needn't handle non-finite values.
Results may differ from the reference program's by a relative error of at most 0.0003.
Values sent between devices are 32-bit elements; how exact they have to be, the bound alone decides.
No kernel may reach another device: no remote copies, remote signals or barrier semaphores. Data moves between devices by JAX's collectives and lax.ppermute only.
A program may use at most 64 MiB of HBM per device.

```python
import math
import jax
import jax.numpy as jnp
from jax import lax

FEATURES = 256
NUM_TEXTS = 16384
NUM_GOALS = 32768


def draw_embed_docs(key, part):
    key = jax.random.fold_in(key, 11)
    key_base = jax.random.fold_in(key, 0)
    values = jax.random.normal(key_base, (NUM_TEXTS, FEATURES), jnp.float32) / math.sqrt(FEATURES)
    return jnp.clip(values, -2.0, 2.0)


def draw_embed_targets(key, part):
    key = jax.random.fold_in(key, 12)
    key_base = jax.random.fold_in(key, 0)
    values = jax.random.normal(key_base, (NUM_GOALS, FEATURES), jnp.float32) / math.sqrt(FEATURES)
    return jnp.clip(values, -2.0, 2.0)


def steps_of(stream_key, shape, pieces, low, high):
    loudness, own = 1.0, jax.random.fold_in(stream_key, 6)
    for dim, shards_of in pieces:
        steps = jnp.exp(jax.random.uniform(jax.random.fold_in(own, dim), (shards_of,), jnp.float32, low / len(pieces), high / len(pieces)))
        loudness = loudness * jnp.repeat(steps, shape[dim] // shards_of).reshape([-1 if axis == dim else 1 for axis in range(len(shape))])
    return loudness


def scatter_about(own_key, dims, width, reach, shards=(), dtype=jnp.bfloat16):
    result = width * jax.random.normal(own_key, dims, jnp.float32)
    if shards:
        result = result * steps_of(own_key, dims, shards, -0.22, 0.18)
    return jnp.clip(result, -reach, reach).astype(dtype)


def setup_inputs(seed: int = 0) -> dict:
    streams_of = jax.random.split(jax.random.key(seed), 4)
    embed_docs = draw_embed_docs(jax.random.fold_in(streams_of[3], 71), 0)
    embed_targets = draw_embed_targets(jax.random.fold_in(streams_of[3], 71), 0)
    starting_goal_multiplier = scatter_about(streams_of[2], (NUM_GOALS,), 0.2, 0.8, ((0, 16),), jnp.float32)
    return dict(embed_docs=embed_docs, embed_targets=embed_targets, starting_goal_multiplier=starting_goal_multiplier)


smoothing_epsilon = 0.05


def reference(embed_docs, embed_targets, starting_goal_multiplier):
    block = math.gcd(NUM_TEXTS, 512)
    blocks = NUM_TEXTS // block
    doc_blocks = embed_docs.reshape(blocks, block, FEATURES)
    target_norms = jnp.sum(embed_targets * embed_targets, axis=1)
    highest = lax.Precision.HIGHEST
    scaling_mass = NUM_TEXTS / NUM_GOALS

    def tile_segment(horizontal_items):
        norms = jnp.sum(horizontal_items * horizontal_items, axis=1)
        return norms[:, None] + target_norms[None, :] - 2.0 * jnp.dot(horizontal_items, embed_targets.T, precision=highest)

    def horizontal_softmax_norm(similarity_grid):
        largest = jnp.max(similarity_grid, axis=1)
        return largest + jnp.log(jnp.sum(jnp.exp(similarity_grid - largest[:, None]), axis=1))

    def doc_potential(goal_multiplier):
        def single(horizontal_items):
            return horizontal_softmax_norm((goal_multiplier[None, :] - tile_segment(horizontal_items)) / smoothing_epsilon)
        log_masses = lax.map(single, doc_blocks).reshape(NUM_TEXTS)
        return smoothing_epsilon * math.log(NUM_GOALS) - smoothing_epsilon * log_masses, log_masses

    def target_potential(doc_pot):
        pots = doc_pot.reshape(blocks, block)

        def advance(carry, item):
            horizontal_items, interim_multipliers = item
            similarity_grid = (interim_multipliers[:, None] - tile_segment(horizontal_items)) / smoothing_epsilon
            largest = jnp.maximum(carry[0], jnp.max(similarity_grid, axis=0))
            mass = carry[1] * jnp.exp(carry[0] - largest) + jnp.sum(jnp.exp(similarity_grid - largest[None, :]), axis=0)
            return (largest, mass), None

        start_carry = (jnp.full((NUM_GOALS,), -jnp.inf, jnp.float32), jnp.zeros((NUM_GOALS,), jnp.float32))
        (largest, mass), _ = lax.scan(advance, start_carry, (doc_blocks, pots))
        log_masses = largest + jnp.log(mass)
        return smoothing_epsilon * math.log(NUM_TEXTS) - smoothing_epsilon * log_masses, log_masses

    text_multiplier_early, horizontal_lse_early = doc_potential(starting_goal_multiplier)
    goal_multiplier_early, vertical_lse_early = target_potential(text_multiplier_early)
    text_multiplier_later, horizontal_lse_later = doc_potential(goal_multiplier_early)
    _, vertical_lse_later = target_potential(text_multiplier_later)

    def shaped(vector):
        return vector.reshape(blocks, block)

    def first_pass(carry, item):
        horizontal_items, multiplier_later, log_mass_later = item
        distance_tile = tile_segment(horizontal_items)
        transport_plan_later = jnp.exp((multiplier_later[:, None] - distance_tile) / smoothing_epsilon - vertical_lse_later[None, :])
        text_sensitivity_later = 1.0 - scaling_mass * jnp.sum(transport_plan_later, axis=1)
        horizontal_items_later = jnp.exp((goal_multiplier_early[None, :] - distance_tile) / smoothing_epsilon - log_mass_later[:, None])
        return carry + jnp.sum(text_sensitivity_later[:, None] * horizontal_items_later, axis=0), text_sensitivity_later

    summed, doc_bars = lax.scan(first_pass, jnp.zeros((NUM_GOALS,), jnp.float32),
                                (doc_blocks, shaped(text_multiplier_later), shaped(horizontal_lse_later)))
    target_bar_one = -summed

    def second_pass(carry, item):
        horizontal_items, multiplier_early, multiplier_later, log_mass_early, log_mass_later, text_sensitivity_later = item
        distance_tile = tile_segment(horizontal_items)
        backward_signal = scaling_mass * jnp.exp((multiplier_later[:, None] - distance_tile) / smoothing_epsilon - vertical_lse_later[None, :])
        backward_signal = backward_signal + text_sensitivity_later[:, None] * jnp.exp((goal_multiplier_early[None, :] - distance_tile) / smoothing_epsilon - log_mass_later[:, None])
        transport_plan_early = jnp.exp((multiplier_early[:, None] - distance_tile) / smoothing_epsilon - vertical_lse_early[None, :])
        backward_signal = backward_signal + target_bar_one[None, :] * transport_plan_early
        text_sensitivity_early = -jnp.sum(target_bar_one[None, :] * transport_plan_early, axis=1)
        backward_signal = backward_signal + text_sensitivity_early[:, None] * jnp.exp((starting_goal_multiplier[None, :] - distance_tile) / smoothing_epsilon - log_mass_early[:, None])
        doc_weight = jnp.sum(backward_signal, axis=1)
        grad_rows = 2.0 * (doc_weight[:, None] * horizontal_items - jnp.dot(backward_signal, embed_targets, precision=highest))
        col_weight = carry[0] + jnp.sum(backward_signal, axis=0)
        cross = carry[1] + lax.dot_general(backward_signal, horizontal_items, (((0,), (0,)), ((), ())), precision=highest)
        return (col_weight, cross), grad_rows

    start_carry = (jnp.zeros((NUM_GOALS,), jnp.float32), jnp.zeros((NUM_GOALS, FEATURES), jnp.float32))
    (col_weight, cross), grad_blocks = lax.scan(
        second_pass, start_carry,
        (doc_blocks, shaped(text_multiplier_early), shaped(text_multiplier_later), shaped(horizontal_lse_early), shaped(horizontal_lse_later), doc_bars))
    grad_docs = grad_blocks.reshape(NUM_TEXTS, FEATURES)
    grad_targets = 2.0 * (col_weight[:, None] * embed_targets - cross)
    return grad_docs, grad_targets
```

```python
import math

import jax
import jax.numpy as jnp
from jax import lax
from jax.sharding import PartitionSpec as P

smoothing_epsilon = 0.05
EXPONENT_MAX = 40.0
LOW, HIGH = 1e-25, 1e25
FIRST_LOW = 1e-9


def row_log_mass(scores):
    largest = lax.pmax(jnp.max(scores, axis=1), "col")
    mass_all = lax.psum(jnp.sum(jnp.exp(scores - largest[:, None]), axis=1), "col")
    return largest + jnp.log(mass_all)


def column_log_mass(scores):
    largest = lax.pmax(jnp.max(scores, axis=0), "row")
    mass_all = lax.psum(jnp.sum(jnp.exp(scores - largest[None, :]), axis=0), "row")
    return largest + jnp.log(mass_all)


def log_domain(embed_docs, embed_targets, doc_block, target_block, start):
    highest = lax.Precision.HIGHEST
    distance_tile = (
        jnp.sum(doc_block * doc_block, axis=1)[:, None]
        + jnp.sum(target_block * target_block, axis=1)[None, :]
        - 2.0 * jnp.dot(doc_block, target_block.T, precision=highest)
    )
    texts = distance_tile.shape[0] * lax.axis_size("row")
    goals = distance_tile.shape[1] * lax.axis_size("col")
    ratio = texts / goals
    t = smoothing_epsilon
    row_log_one = row_log_mass((start[None, :] - distance_tile) / t)
    doc_one = t * math.log(goals) - t * row_log_one
    col_log_one = column_log_mass((doc_one[:, None] - distance_tile) / t)
    target_one = t * math.log(texts) - t * col_log_one
    row_log_two = row_log_mass((target_one[None, :] - distance_tile) / t)
    doc_two = t * math.log(goals) - t * row_log_two
    col_log_two = column_log_mass((doc_two[:, None] - distance_tile) / t)
    plan = jnp.exp((doc_two[:, None] - distance_tile) / t - col_log_two[None, :])
    adjoint = ratio * plan
    doc_bar_two = 1.0 - ratio * lax.psum(jnp.sum(plan, axis=1), "col")
    plan = jnp.exp((target_one[None, :] - distance_tile) / t - row_log_two[:, None])
    weighted = doc_bar_two[:, None] * plan
    adjoint = adjoint + weighted
    target_bar_one = -lax.psum(jnp.sum(weighted, axis=0), "row")
    plan = jnp.exp((doc_one[:, None] - distance_tile) / t - col_log_one[None, :])
    weighted = target_bar_one[None, :] * plan
    adjoint = adjoint + weighted
    doc_bar_one = -lax.psum(jnp.sum(weighted, axis=1), "col")
    plan = jnp.exp((start[None, :] - distance_tile) / t - row_log_one[:, None])
    adjoint = adjoint + doc_bar_one[:, None] * plan
    doc_part = 2.0 * (
        jnp.sum(adjoint, axis=1)[:, None] * doc_block
        - jnp.dot(adjoint, target_block, precision=highest)
    )
    crossed = lax.dot_general(adjoint, doc_block, (((0,), (0,)), ((), ())), precision=highest)
    target_part = 2.0 * (jnp.sum(adjoint, axis=0)[:, None] * target_block - crossed)
    share, target_share = embed_docs.shape[0], embed_targets.shape[0]
    doc_whole, target_whole = lax.psum(doc_part, "col"), lax.psum(target_part, "row")
    return (
        lax.dynamic_slice_in_dim(doc_whole, lax.axis_index("col") * share, share, 0),
        lax.dynamic_slice_in_dim(
            target_whole, lax.axis_index("row") * target_share, target_share, 0
        ),
    )


def swap(blocks, axis):
    return lax.all_to_all(blocks, axis, 0, 0)


def gather(block, axis):
    devices = lax.axis_size(axis)
    pieces = swap(jnp.broadcast_to(block[None], (devices, *block.shape)), axis)
    return pieces.reshape(devices * block.shape[0], *block.shape[1:])


def total(vector, axis):
    return jnp.sum(swap(jnp.broadcast_to(vector[None], (lax.axis_size(axis), *vector.shape)), axis), axis=0)


def scatter(block, axis):
    devices = lax.axis_size(axis)
    pieces = block.reshape(devices, block.shape[0] // devices, *block.shape[1:])
    return jnp.sum(swap(pieces, axis), axis=0)


def inverse(mass, low, high):
    return jnp.where((mass >= low) & (mass <= high), 1.0 / mass, jnp.nan)


def local(embed_docs, embed_targets, start):
    t = smoothing_epsilon
    high = lax.Precision.HIGH
    targets = gather(embed_targets, "row")
    docs = gather(embed_docs, "col")
    texts, goals = docs.shape[0] * lax.axis_size("row"), targets.shape[0] * lax.axis_size("col")
    ratio = texts / goals
    exponent = (2.0 / t) * jnp.dot(docs, targets.T, precision=high)
    fits = jnp.max(jnp.abs(exponent)) <= EXPONENT_MAX
    kernel = jnp.exp(exponent)

    def rows(weight):
        return total(jnp.sum(kernel * weight[None, :], axis=1), "col")

    def columns(weight):
        return total(jnp.sum(kernel * weight[:, None], axis=0), "row")

    target_zero = jnp.exp((start - jnp.sum(targets * targets, axis=1)) / t)
    target_zero = jnp.where(fits, target_zero, jnp.nan)
    doc_one = inverse(rows(target_zero), FIRST_LOW, HIGH)
    target_one = inverse(columns(doc_one), LOW, HIGH)
    doc_two = inverse(rows(target_one), LOW, HIGH)
    target_two = inverse(columns(doc_two), LOW, HIGH)
    mass = rows(target_two)
    doc_bar_two = 1.0 - ratio * doc_two * mass
    weighted_two = doc_two * doc_bar_two
    weighted_one = -target_one * target_one * columns(weighted_two)
    weighted_zero = -doc_one * doc_one * rows(weighted_one)
    first = weighted_zero[:, None] * target_zero[None, :]
    adjoint = kernel * (
        ratio * doc_two[:, None] * target_two[None, :]
        + weighted_two[:, None] * target_one[None, :]
        + doc_one[:, None] * weighted_one[None, :]
        + first
    )
    column_mass = ratio / lax.axis_size("row") + jnp.sum(kernel * first, axis=0)
    doc_part = jnp.dot(adjoint, targets, precision=high)
    crossed = lax.dot_general(adjoint, docs, (((0,), (0,)), ((), ())), precision=high)
    grad_docs = 2.0 * (embed_docs - scatter(doc_part, "col"))
    grad_targets = scatter(2.0 * (column_mass[:, None] * targets - crossed), "row")
    return lax.cond(
        jnp.isnan(jnp.sum(mass)),
        lambda: log_domain(embed_docs, embed_targets, docs, targets, start),
        lambda: (grad_docs, grad_targets),
    )


def solution(mesh):
    return jax.shard_map(
        local,
        mesh=mesh,
        in_specs=(P(("row", "col"), None), P(("col", "row"), None), P("col")),
        out_specs=(P(("row", "col"), None), P(("col", "row"), None)),
        check_vma=False,
    )
```

```python
import math
from functools import partial

import jax
import jax.numpy as jnp
from jax import lax
from jax.experimental import pallas as pl
from jax.experimental.pallas import tpu as pltpu
from jax.sharding import PartitionSpec as P

smoothing_epsilon = 0.05
EXPONENT_MAX = 40.0
LOW, HIGH = 1e-25, 1e25
FIRST_LOW = 1e-9
KEPT, HELD = (0,), (0,)


def row_log_mass(scores):
    largest = lax.pmax(jnp.max(scores, axis=1), "col")
    mass_all = lax.psum(jnp.sum(jnp.exp(scores - largest[:, None]), axis=1), "col")
    return largest + jnp.log(mass_all)


def column_log_mass(scores):
    largest = lax.pmax(jnp.max(scores, axis=0), "row")
    mass_all = lax.psum(jnp.sum(jnp.exp(scores - largest[None, :]), axis=0), "row")
    return largest + jnp.log(mass_all)


def log_domain(doc_block, target_block, start):
    highest = lax.Precision.HIGHEST
    distance_tile = (
        jnp.sum(doc_block * doc_block, axis=1)[:, None]
        + jnp.sum(target_block * target_block, axis=1)[None, :]
        - 2.0 * jnp.dot(doc_block, target_block.T, precision=highest)
    )
    texts = distance_tile.shape[0] * lax.axis_size("row")
    goals = distance_tile.shape[1] * lax.axis_size("col")
    ratio = texts / goals
    t = smoothing_epsilon
    row_log_one = row_log_mass((start[None, :] - distance_tile) / t)
    doc_one = t * math.log(goals) - t * row_log_one
    col_log_one = column_log_mass((doc_one[:, None] - distance_tile) / t)
    target_one = t * math.log(texts) - t * col_log_one
    row_log_two = row_log_mass((target_one[None, :] - distance_tile) / t)
    doc_two = t * math.log(goals) - t * row_log_two
    col_log_two = column_log_mass((doc_two[:, None] - distance_tile) / t)
    plan = jnp.exp((doc_two[:, None] - distance_tile) / t - col_log_two[None, :])
    adjoint = ratio * plan
    doc_bar_two = 1.0 - ratio * lax.psum(jnp.sum(plan, axis=1), "col")
    plan = jnp.exp((target_one[None, :] - distance_tile) / t - row_log_two[:, None])
    weighted = doc_bar_two[:, None] * plan
    adjoint = adjoint + weighted
    target_bar_one = -lax.psum(jnp.sum(weighted, axis=0), "row")
    plan = jnp.exp((doc_one[:, None] - distance_tile) / t - col_log_one[None, :])
    weighted = target_bar_one[None, :] * plan
    adjoint = adjoint + weighted
    doc_bar_one = -lax.psum(jnp.sum(weighted, axis=1), "col")
    plan = jnp.exp((start[None, :] - distance_tile) / t - row_log_one[:, None])
    adjoint = adjoint + doc_bar_one[:, None] * plan
    doc_part = 2.0 * (
        jnp.sum(adjoint, axis=1)[:, None] * doc_block
        - jnp.dot(adjoint, target_block, precision=highest)
    )
    crossed = lax.dot_general(adjoint, doc_block, (((0,), (0,)), ((), ())), precision=highest)
    target_part = 2.0 * (jnp.sum(adjoint, axis=0)[:, None] * target_block - crossed)
    return scatter(doc_part, "col"), scatter(target_part, "row")


LANES = 128
f32, bf16 = jnp.float32, jnp.bfloat16


def swap(blocks, axis):
    return lax.all_to_all(blocks, axis, 0, 0)


def gather(block, axis):
    devices = lax.axis_size(axis)
    pieces = swap(jnp.broadcast_to(block[None], (devices, *block.shape)), axis)
    return pieces.reshape(devices * block.shape[0], *block.shape[1:])


def scatter(block, axis):
    devices = lax.axis_size(axis)
    pieces = block.reshape(devices, block.shape[0] // devices, *block.shape[1:])
    return jnp.sum(swap(pieces, axis), axis=0)


def inverse(mass, low, high):
    return jnp.where((mass >= low) & (mass <= high), 1.0 / mass, jnp.nan)


def halves(values):
    top = values.astype(bf16)
    return top, (values - top.astype(f32)).astype(bf16)


def spans(size, step):
    return [slice(i, i + step) for i in range(0, size, step)]


def upright(vector):
    return jnp.transpose(jnp.broadcast_to(vector, (LANES, LANES)))


def lane_total(block):
    return jnp.sum(jnp.transpose(block), axis=0, keepdims=True)


def row_sums(tile, weight):
    out = []
    for rows in spans(tile.shape[0], LANES):
        acc = None
        for c, cols in enumerate(spans(tile.shape[1], LANES)):
            term = tile[rows, cols] * weight[c : c + 1, :]
            acc = term if acc is None else acc + term
        out.append(lane_total(acc))
    return jnp.concatenate(out, axis=0)


def column_sums(tile, weight):
    columns = spans(tile.shape[1], LANES)
    acc = [None] * len(columns)
    for r, rows in enumerate(spans(tile.shape[0], LANES)):
        factor = upright(weight[r : r + 1, :])
        for c, cols in enumerate(columns):
            term = jnp.sum((tile[rows, cols] * factor).reshape(-1, 8, LANES), axis=0)
            acc[c] = term if acc[c] is None else acc[c] + term
    return jnp.concatenate([jnp.sum(a, axis=0, keepdims=True) for a in acc], axis=0)


def spread(ref, values):
    ref[...] = jnp.broadcast_to(values[None], ref.shape)


def kernel_tile(docs, targets, start, tile, weight_out, part, doc_wide, target_wide):
    features = docs.shape[1]
    for source, wide, order in ((docs, doc_wide, (0, 0, 1)), (targets, target_wide, (0, 1, 0))):
        for rows in spans(source.shape[0], 256):
            pair = halves(source[rows, :])
            for k, which in enumerate(order):
                wide[rows, k * features : (k + 1) * features] = pair[which]
    largest = None
    for cols in spans(targets.shape[0], 256):
        dots = lax.dot_general(
            doc_wide[...], target_wide[cols, :], (((1,), (1,)), ((), ())), preferred_element_type=f32
        )
        dots = dots * (2.0 / smoothing_epsilon)
        tile[:, cols] = jnp.exp(dots)
        peak = jnp.max(jnp.abs(dots).reshape(-1, 8, 256), axis=0)
        largest = peak if largest is None else jnp.maximum(largest, peak)
    fits = jnp.max(largest) <= EXPONENT_MAX
    norms = []
    for rows in spans(targets.shape[0], LANES):
        squares = targets[rows, :] * targets[rows, :]
        norms.append(lane_total(sum(squares[:, cols] for cols in spans(features, LANES))))
    weight = jnp.exp((start[...] - jnp.concatenate(norms, axis=0)) / smoothing_epsilon)
    weight = jnp.where(fits, weight, jnp.nan)
    weight_out[...] = weight
    spread(part, row_sums(tile, weight))


def kernel_doc_one(tile, parts, weight_out, part):
    weight = inverse(jnp.sum(parts[...], axis=0), FIRST_LOW, HIGH)
    weight_out[...] = weight
    spread(part, column_sums(tile, weight))


def kernel_doc_two(tile, parts, weight_out, part):
    weight = inverse(jnp.sum(parts[...], axis=0), LOW, HIGH)
    weight_out[...] = weight
    spread(part, column_sums(tile, weight))


def kernel_target(tile, parts, weight_out, part):
    weight = inverse(jnp.sum(parts[...], axis=0), LOW, HIGH)
    weight_out[...] = weight
    spread(part, row_sums(tile, weight))


def kernel_bar_two(ratio, tile, parts, doc_two, weight_out, part):
    scale = doc_two[...]
    weight = scale * (1.0 - ratio * scale * jnp.sum(parts[...], axis=0))
    weight_out[...] = weight
    spread(part, column_sums(tile, weight))


def kernel_bar_one(tile, parts, target_one, weight_out, part):
    scale = target_one[...]
    weight = -scale * scale * jnp.sum(parts[...], axis=0)
    weight_out[...] = weight
    spread(part, row_sums(tile, weight))


def kernel_docs(ratio, tile, parts, doc_one, doc_two, bar_two, target_zero, target_one, target_two, bar_one,
                targets, top, low, mass, doc_part, factors, wide):
    features = targets.shape[1]
    for rows in spans(targets.shape[0], 256):
        pair = halves(targets[rows, :])
        wide[rows, :features], wide[rows, features:] = pair
    one = doc_one[...]
    bar_zero = -one * one * jnp.sum(parts[...], axis=0)
    by_row = (bar_zero, ratio * doc_two[...], bar_two[...], one)
    by_column = (target_zero[...], target_two[...], target_one[...], bar_one[...])
    columns = spans(tile.shape[1], LANES)
    acc = [None] * len(columns)
    for r, rows in enumerate(spans(tile.shape[0], LANES)):
        for k, values in enumerate(by_row):
            factors[k, rows, :] = upright(values[r : r + 1, :])
    for block in spans(tile.shape[0], 256):
        for rows in spans(256, 32):
            rows = slice(block.start + rows.start, block.start + rows.stop)
            a = [factors[k, rows, :] for k in range(4)]
            for c, cols in enumerate(columns):
                b = [v[c : c + 1, :] for v in by_column]
                adjoint = tile[rows, cols] * ((a[0] * b[0] + a[1] * b[1]) + (a[2] * b[2] + a[3] * b[3]))
                term = jnp.sum(adjoint.reshape(-1, 8, LANES), axis=0)
                acc[c] = term if acc[c] is None else acc[c] + term
                top[rows, cols], low[rows, cols] = halves(adjoint)
        both = jnp.dot(top[block, :], wide[...], preferred_element_type=f32)
        rest = jnp.dot(low[block, :], wide[:, :features], preferred_element_type=f32)
        doc_part[block, :] = (both[:, :features] + both[:, features:]) + rest
    mass[...] = jnp.concatenate([jnp.sum(a, axis=0, keepdims=True) for a in acc], axis=0)


def kernel_targets(top, low, mass, docs, targets, target_part, flat):
    features = docs.shape[1]
    for rows in spans(docs.shape[0], 256):
        pair = halves(jnp.transpose(docs[rows, :]))
        flat[:features, rows], flat[features:, rows] = pair
    for cols in spans(targets.shape[0], 256):
        both = jnp.dot(flat[...], top[:, cols], preferred_element_type=f32)
        rest = jnp.dot(flat[:features, :], low[:, cols], preferred_element_type=f32)
        crossed = jnp.transpose((both[:features] + both[features:]) + rest)
        for k, rows in enumerate(spans(256, LANES)):
            r = cols.start // LANES + k
            here = slice(cols.start + rows.start, cols.start + rows.stop)
            weight = upright(mass[r : r + 1, :])
            for half in spans(features, LANES):
                target_part[here, half] = 2.0 * (weight * targets[here, half] - crossed[rows, half])


def run(kernel, args, outs, scratch=(), limit=16, held=(), kept=()):
    args = [pltpu.with_memory_space_constraint(a, pltpu.VMEM) if i in held else a for i, a in enumerate(args)]
    shapes = [pltpu.VMEM(*o) if i in kept else jax.ShapeDtypeStruct(*o) for i, o in enumerate(outs)]
    return pl.pallas_call(
        kernel,
        out_shape=shapes,
        in_specs=[pl.BlockSpec(memory_space=pltpu.VMEM)] * len(args),
        out_specs=[pl.BlockSpec(memory_space=pltpu.VMEM)] * len(outs),
        scratch_shapes=[pltpu.VMEM(*s) for s in scratch],
        compiler_params=pltpu.CompilerParams(vmem_limit_bytes=limit << 20),
    )(*args)


def local(embed_docs, embed_targets, start):
    targets = gather(embed_targets, "row")
    docs = gather(embed_docs, "col")
    (n, features), m = docs.shape, targets.shape[0]
    rows, cols = lax.axis_size("row"), lax.axis_size("col")
    ratio = (n * rows) / (m * cols)
    doc_vector, target_vector = ((n // LANES, LANES), f32), ((m // LANES, LANES), f32)
    doc_parts, target_parts = ((cols, *doc_vector[0]), f32), ((rows, *target_vector[0]), f32)
    tile, target_zero, part = run(
        kernel_tile,
        (docs, targets, start.reshape(target_vector[0])),
        [((n, m), f32), target_vector, doc_parts],
        [((n, 3 * features), bf16), ((m, 3 * features), bf16)],
        limit=24, kept=KEPT,
    )

    def step(kernel, part, axis, *extra, over_docs):
        outs = [doc_vector, target_parts] if over_docs else [target_vector, doc_parts]
        return run(kernel, (tile, swap(part, axis), *extra), outs, held=HELD)

    doc_one, part = step(kernel_doc_one, part, "col", over_docs=True)
    target_one, part = step(kernel_target, part, "row", over_docs=False)
    doc_two, part = step(kernel_doc_two, part, "col", over_docs=True)
    target_two, part = step(kernel_target, part, "row", over_docs=False)
    bar_two, part = step(partial(kernel_bar_two, ratio), part, "col", doc_two, over_docs=True)
    bar_one, part = step(kernel_bar_one, part, "row", target_one, over_docs=False)
    top, low, mass, doc_part = run(
        partial(kernel_docs, ratio),
        (tile, swap(part, "col"), doc_one, doc_two, bar_two, target_zero, target_one, target_two, bar_one, targets),
        [((n, m), bf16), ((n, m), bf16), target_vector, ((n, features), f32)],
        [((4, n, LANES), f32), ((m, 2 * features), bf16)],
        limit=32, held=HELD, kept=(0, 1),
    )
    (target_part,) = run(
        kernel_targets, (top, low, mass, docs, targets), [((m, features), f32)], [((2 * features, n), bf16)],
        limit=24, held=(0, 1),
    )
    grad_docs = 2.0 * (embed_docs - scatter(doc_part, "col"))
    grad_targets = scatter(target_part, "row")
    return lax.cond(
        jnp.isnan(jnp.sum(bar_two)),
        lambda: log_domain(docs, targets, start),
        lambda: (grad_docs, grad_targets),
    )


def solution(mesh):
    return jax.shard_map(
        local,
        mesh=mesh,
        in_specs=(P(("row", "col"), None), P(("col", "row"), None), P("col")),
        out_specs=(P(("row", "col"), None), P(("col", "row"), None)),
        check_vma=False,
    )
```

```python
import math
from functools import partial

import jax
import jax.numpy as jnp
from jax import lax
from jax.experimental import pallas as pl
from jax.experimental.pallas import tpu as pltpu
from jax.sharding import PartitionSpec as P

smoothing_epsilon = 0.05
EXPONENT_MAX = 40.0
LOW, HIGH = 1e-25, 1e25
FIRST_LOW = 1e-9
KEPT, HELD = (0,), (0,)
ROW, COL = ("z_lo", "x", "core"), ("y", "z_hi")
SIZES = {"z_lo": 2, "x": 4, "core": 2, "y": 4, "z_hi": 4}


def row_log_mass(scores):
    largest = lax.pmax(jnp.max(scores, axis=1), COL)
    mass_all = lax.psum(jnp.sum(jnp.exp(scores - largest[:, None]), axis=1), COL)
    return largest + jnp.log(mass_all)


def column_log_mass(scores):
    largest = lax.pmax(jnp.max(scores, axis=0), ROW)
    mass_all = lax.psum(jnp.sum(jnp.exp(scores - largest[None, :]), axis=0), ROW)
    return largest + jnp.log(mass_all)


def log_domain(embed_docs, embed_targets, start):
    doc_block, target_block = gather(embed_docs, COL), gather(embed_targets, ROW)
    highest = lax.Precision.HIGHEST
    distance_tile = (
        jnp.sum(doc_block * doc_block, axis=1)[:, None]
        + jnp.sum(target_block * target_block, axis=1)[None, :]
        - 2.0 * jnp.dot(doc_block, target_block.T, precision=highest)
    )
    texts = distance_tile.shape[0] * lax.axis_size(ROW)
    goals = distance_tile.shape[1] * lax.axis_size(COL)
    ratio = texts / goals
    t = smoothing_epsilon
    row_log_one = row_log_mass((start[None, :] - distance_tile) / t)
    doc_one = t * math.log(goals) - t * row_log_one
    col_log_one = column_log_mass((doc_one[:, None] - distance_tile) / t)
    target_one = t * math.log(texts) - t * col_log_one
    row_log_two = row_log_mass((target_one[None, :] - distance_tile) / t)
    doc_two = t * math.log(goals) - t * row_log_two
    col_log_two = column_log_mass((doc_two[:, None] - distance_tile) / t)
    plan = jnp.exp((doc_two[:, None] - distance_tile) / t - col_log_two[None, :])
    adjoint = ratio * plan
    doc_bar_two = 1.0 - ratio * lax.psum(jnp.sum(plan, axis=1), COL)
    plan = jnp.exp((target_one[None, :] - distance_tile) / t - row_log_two[:, None])
    weighted = doc_bar_two[:, None] * plan
    adjoint = adjoint + weighted
    target_bar_one = -lax.psum(jnp.sum(weighted, axis=0), ROW)
    plan = jnp.exp((doc_one[:, None] - distance_tile) / t - col_log_one[None, :])
    weighted = target_bar_one[None, :] * plan
    adjoint = adjoint + weighted
    doc_bar_one = -lax.psum(jnp.sum(weighted, axis=1), COL)
    plan = jnp.exp((start[None, :] - distance_tile) / t - row_log_one[:, None])
    adjoint = adjoint + doc_bar_one[:, None] * plan
    doc_part = 2.0 * (
        jnp.sum(adjoint, axis=1)[:, None] * doc_block
        - jnp.dot(adjoint, target_block, precision=highest)
    )
    crossed = lax.dot_general(adjoint, doc_block, (((0,), (0,)), ((), ())), precision=highest)
    target_part = 2.0 * (jnp.sum(adjoint, axis=0)[:, None] * target_block - crossed)
    return scatter(doc_part, COL), scatter(target_part, ROW)


LANES = 128
f32, bf16 = jnp.float32, jnp.bfloat16


def swap(blocks, axis):
    return lax.all_to_all(blocks, axis, 0, 0)


def gather(block, axis):
    devices = lax.axis_size(axis)
    pieces = swap(jnp.broadcast_to(block[None], (devices, *block.shape)), axis)
    return pieces.reshape(devices * block.shape[0], *block.shape[1:])


def scatter(block, axis):
    devices = lax.axis_size(axis)
    pieces = block.reshape(devices, block.shape[0] // devices, *block.shape[1:])
    return jnp.sum(swap(pieces, axis), axis=0)


def inverse(mass, low, high):
    return jnp.where((mass >= low) & (mass <= high), 1.0 / mass, jnp.nan)


def halves(values):
    top = values.astype(bf16)
    return top, (values - top.astype(f32)).astype(bf16)


def spans(size, step):
    return [slice(i, i + step) for i in range(0, size, step)]


def upright(vector):
    return jnp.transpose(jnp.broadcast_to(vector, (LANES, LANES)))


def lane_total(block):
    return jnp.sum(jnp.transpose(block), axis=0, keepdims=True)


def row_sums(tile, weight):
    out = []
    for rows in spans(tile.shape[0], LANES):
        acc = None
        for c, cols in enumerate(spans(tile.shape[1], LANES)):
            term = tile[rows, cols] * weight[c : c + 1, :]
            acc = term if acc is None else acc + term
        out.append(lane_total(acc))
    return jnp.concatenate(out, axis=0)


def column_sums(tile, weight):
    columns = spans(tile.shape[1], LANES)
    acc = [None] * len(columns)
    for r, rows in enumerate(spans(tile.shape[0], LANES)):
        factor = upright(weight[r : r + 1, :])
        for c, cols in enumerate(columns):
            term = jnp.sum((tile[rows, cols] * factor).reshape(-1, 8, LANES), axis=0)
            acc[c] = term if acc[c] is None else acc[c] + term
    return jnp.concatenate([jnp.sum(a, axis=0, keepdims=True) for a in acc], axis=0)


def spread(ref, values):
    ref[...] = jnp.broadcast_to(values[None], ref.shape)


def turned(place, by, size):
    return lax.rem(place + by, size)


def kernel_tile(place, start, near, *refs):
    far, (mine, other), (docs, targets, tile, weight_out, part, doc_wide, target_wide) = refs[:-9], refs[-9:-7], refs[-7:]
    features = docs.shape[1]
    sizes = SIZES["y"], SIZES["z_hi"]
    share = docs.shape[0] // (sizes[0] * sizes[1])
    for k, source in enumerate((near, *far)):
        y = turned(place[0], sizes[0] - k, sizes[0])
        for j in range(sizes[1]):
            at = (y * sizes[1] + turned(place[1], sizes[1] - j, sizes[1])) * share
            docs[pl.ds(pl.multiple_of(at, share), share), :] = source[j * share : (j + 1) * share, :]
    half = mine.shape[0]
    targets[pl.ds(pl.multiple_of(place[2] * half, half), half), :] = mine[...]
    targets[pl.ds(pl.multiple_of((1 - place[2]) * half, half), half), :] = other[...]
    for source, wide, order in ((docs, doc_wide, (0, 0, 1)), (targets, target_wide, (0, 1, 0))):
        for rows in spans(source.shape[0], 256):
            pair = halves(source[rows, :])
            for k, which in enumerate(order):
                wide[rows, k * features : (k + 1) * features] = pair[which]
    largest = None
    for cols in spans(targets.shape[0], 256):
        dots = lax.dot_general(
            doc_wide[...], target_wide[cols, :], (((1,), (1,)), ((), ())), preferred_element_type=f32
        )
        dots = dots * (2.0 / smoothing_epsilon)
        tile[:, cols] = jnp.exp(dots)
        peak = jnp.max(jnp.abs(dots).reshape(-1, 8, 256), axis=0)
        largest = peak if largest is None else jnp.maximum(largest, peak)
    fits = jnp.max(largest) <= EXPONENT_MAX
    norms = []
    for rows in spans(targets.shape[0], LANES):
        squares = targets[rows, :] * targets[rows, :]
        norms.append(lane_total(sum(squares[:, cols] for cols in spans(features, LANES))))
    count = start.shape[0]
    begin = jnp.concatenate([start[i : i + 1, :] for c in range(2) for i in range(c, count, 2)], axis=0)
    weight = jnp.exp((begin - jnp.concatenate(norms, axis=0)) / smoothing_epsilon)
    weight = jnp.where(fits, weight, jnp.nan)
    weight_out[...] = weight
    spread(part, row_sums(tile, weight))


def kernel_doc_one(tile, parts, weight_out, part):
    weight = inverse(jnp.sum(parts[...], axis=0), FIRST_LOW, HIGH)
    weight_out[...] = weight
    spread(part, column_sums(tile, weight))


def kernel_doc_two(tile, parts, weight_out, part):
    weight = inverse(jnp.sum(parts[...], axis=0), LOW, HIGH)
    weight_out[...] = weight
    spread(part, column_sums(tile, weight))


def kernel_target(tile, parts, weight_out, part):
    weight = inverse(jnp.sum(parts[...], axis=0), LOW, HIGH)
    weight_out[...] = weight
    spread(part, row_sums(tile, weight))


def kernel_bar_two(ratio, tile, parts, doc_two, weight_out, part):
    scale = doc_two[...]
    weight = scale * (1.0 - ratio * scale * jnp.sum(parts[...], axis=0))
    weight_out[...] = weight
    spread(part, column_sums(tile, weight))


def kernel_bar_one(tile, parts, target_one, weight_out, part):
    scale = target_one[...]
    weight = -scale * scale * jnp.sum(parts[...], axis=0)
    weight_out[...] = weight
    spread(part, row_sums(tile, weight))


def kernel_docs(ratio, place, tile, parts, doc_one, doc_two, bar_two, target_zero, target_one, target_two, bar_one,
                targets, top, low, mass, *refs):
    pieces, (factors, wide) = refs[:-2], refs[-2:]
    features = targets.shape[1]
    for rows in spans(targets.shape[0], 256):
        pair = halves(targets[rows, :])
        wide[rows, :features], wide[rows, features:] = pair
    one = doc_one[...]
    bar_zero = -one * one * jnp.sum(parts[...], axis=0)
    by_row = (bar_zero, ratio * doc_two[...], bar_two[...], one)
    by_column = (target_zero[...], target_two[...], target_one[...], bar_one[...])
    columns = spans(tile.shape[1], LANES)
    acc = [None] * len(columns)
    for r, rows in enumerate(spans(tile.shape[0], LANES)):
        for k, values in enumerate(by_row):
            factors[k, rows, :] = upright(values[r : r + 1, :])
    size = pieces[0].shape[0]
    for k, piece in enumerate(pieces):
        first = pl.multiple_of(turned(place[0], k, len(pieces)) * size, size)
        for rows in spans(size, 32):
            rows = pl.ds(first + rows.start, 32)
            a = [factors[i, rows, :] for i in range(4)]
            for c, cols in enumerate(columns):
                b = [v[c : c + 1, :] for v in by_column]
                adjoint = tile[rows, cols] * ((a[0] * b[0] + a[1] * b[1]) + (a[2] * b[2] + a[3] * b[3]))
                term = jnp.sum(adjoint.reshape(-1, 8, LANES), axis=0)
                acc[c] = term if acc[c] is None else acc[c] + term
                top[rows, cols], low[rows, cols] = halves(adjoint)
        block = pl.ds(first, size)
        both = jnp.dot(top[block, :], wide[...], preferred_element_type=f32)
        rest = jnp.dot(low[block, :], wide[:, :features], preferred_element_type=f32)
        piece[...] = (both[:, :features] + both[:, features:]) + rest
    mass[...] = jnp.concatenate([jnp.sum(a, axis=0, keepdims=True) for a in acc], axis=0)


def kernel_targets(place, top, low, mass, docs, targets, other, mine, flat):
    features = docs.shape[1]
    for rows in spans(docs.shape[0], 256):
        pair = halves(jnp.transpose(docs[rows, :]))
        flat[:features, rows], flat[features:, rows] = pair
    half = mine.shape[0]
    for core, out in ((1 - place[2], other), (place[2], mine)):
        for inner in spans(half, 256):
            first = pl.multiple_of(core * half + inner.start, 256)
            cols = pl.ds(first, 256)
            both = jnp.dot(flat[...], top[:, cols], preferred_element_type=f32)
            rest = jnp.dot(flat[:features, :], low[:, cols], preferred_element_type=f32)
            crossed = jnp.transpose((both[:features] + both[features:]) + rest)
            for rows in spans(256, LANES):
                at = core * (half // LANES) + (inner.start + rows.start) // LANES
                weight = upright(mass[pl.ds(at, 1), :])
                here = pl.ds(first + rows.start, LANES)
                for part in spans(features, LANES):
                    out[inner.start + rows.start : inner.start + rows.stop, part] = 2.0 * (
                        weight * targets[here, part] - crossed[rows, part]
                    )


def kernel_pieces(place, *refs):
    parts, pieces = refs[: SIZES["y"]], refs[SIZES["y"] :]
    size = pieces[0].shape[0]
    for k, piece in enumerate(pieces):
        rows = pl.ds(pl.multiple_of(turned(place[1], k, len(pieces)) * size, size), size)
        piece[...] = sum(part[rows, :] for part in parts)


def kernel_pair(one, two, out):
    out[...] = one[...] + two[...]


def kernel_grads(own, *refs):
    parts, (blocks, grad_docs, grad_targets) = refs[:-3], refs[-3:]
    grad_docs[...] = 2.0 * (own[...] - sum(part[...] for part in parts))
    grad_targets[...] = jnp.sum(blocks[...], axis=0)


def run(kernel, args, outs, scratch=(), limit=16, held=(), kept=(), flops=0, place=None):
    args = [pltpu.with_memory_space_constraint(a, pltpu.VMEM) if i in held else a for i, a in enumerate(args)]
    shapes = [pltpu.VMEM(*o) if i in kept else jax.ShapeDtypeStruct(*o) for i, o in enumerate(outs)]
    whole = pl.BlockSpec(memory_space=pltpu.VMEM)
    specs = [whole] * len(args)
    if place is not None:
        args, specs = [place, *args], [pl.BlockSpec(memory_space=pltpu.SMEM), *specs]
    size = sum(math.prod(a.shape) * a.dtype.itemsize for a in args)
    return pl.pallas_call(
        kernel,
        out_shape=shapes,
        in_specs=specs,
        out_specs=[whole] * len(outs),
        scratch_shapes=[pltpu.VMEM(*s) for s in scratch],
        compiler_params=pltpu.CompilerParams(vmem_limit_bytes=limit << 20),
        cost_estimate=pl.CostEstimate(flops=flops, bytes_accessed=size, transcendentals=0),
    )(*args)


def ring(blocks, axis):
    size = SIZES[axis]
    return [
        block if k == 0 else lax.ppermute(block, axis, [(i, (i + k) % size) for i in range(size)])
        for k, block in enumerate(blocks)
    ]


def local(embed_docs, embed_targets, start):
    rows, cols = lax.axis_size(ROW), lax.axis_size(COL)
    place = jnp.stack([lax.axis_index(a) for a in ("y", "z_hi", "core")]).astype(jnp.int32)
    mine = gather(embed_targets, ("z_lo", "x"))
    other = lax.ppermute(mine, "core", [(0, 1), (1, 0)])
    near = jnp.concatenate(ring([embed_docs] * SIZES["z_hi"], "z_hi"), axis=0)
    doc_pieces = ring([near] * SIZES["y"], "y")
    (share, features), (target_share, _) = embed_docs.shape, embed_targets.shape
    n, m = share * cols, target_share * rows
    ratio = (n * rows) / (m * cols)
    product = 6 * n * m * features
    doc_vector, target_vector = ((n // LANES, LANES), f32), ((m // LANES, LANES), f32)
    doc_parts, target_parts = ((cols, *doc_vector[0]), f32), ((rows, *target_vector[0]), f32)
    docs, targets, tile, target_zero, part = run(
        kernel_tile,
        (start.reshape(target_vector[0]), *doc_pieces, mine, other),
        [((n, features), f32), ((m, features), f32), ((n, m), f32), target_vector, doc_parts],
        [((n, 3 * features), bf16), ((m, 3 * features), bf16)],
        limit=28, kept=(2,), flops=product, place=place,
    )

    def step(kernel, part, axis, *extra, over_docs):
        outs = [doc_vector, target_parts] if over_docs else [target_vector, doc_parts]
        return run(kernel, (tile, swap(part, axis), *extra), outs, held=HELD, flops=2 * n * m)

    doc_one, part = step(kernel_doc_one, part, COL, over_docs=True)
    target_one, part = step(kernel_target, part, ROW, over_docs=False)
    doc_two, part = step(kernel_doc_two, part, COL, over_docs=True)
    target_two, part = step(kernel_target, part, ROW, over_docs=False)
    bar_two, part = step(partial(kernel_bar_two, ratio), part, COL, doc_two, over_docs=True)
    bar_one, part = step(kernel_bar_one, part, ROW, target_one, over_docs=False)
    top, low, mass, *doc_pieces = run(
        partial(kernel_docs, ratio),
        (tile, swap(part, COL), doc_one, doc_two, bar_two, target_zero, target_one, target_two, bar_one, targets),
        [((n, m), bf16), ((n, m), bf16), target_vector] + [((n // SIZES["y"], features), f32)] * SIZES["y"],
        [((4, n, LANES), f32), ((m, 2 * features), bf16)],
        limit=32, held=HELD, kept=(0, 1), flops=product, place=place,
    )
    doc_pieces = ring(doc_pieces, "y")
    other, mine = run(
        kernel_targets, (top, low, mass, docs, targets), [((m // 2, features), f32)] * 2, [((2 * features, n), bf16)],
        limit=24, held=(0, 1), flops=product, place=place,
    )
    (mine,) = run(kernel_pair, (mine, lax.ppermute(other, "core", [(0, 1), (1, 0)])), [((m // 2, features), f32)])
    doc_pieces = run(kernel_pieces, doc_pieces, [((share, features), f32)] * SIZES["z_hi"], place=place)
    doc_pieces = ring(doc_pieces, "z_hi")
    blocks = swap(mine.reshape(rows // 2, target_share, features), ("z_lo", "x"))
    grads = run(
        kernel_grads, (embed_docs, *doc_pieces, blocks), [((share, features), f32), ((target_share, features), f32)]
    )
    return lax.cond(
        jnp.isnan(jnp.sum(bar_two)),
        lambda: log_domain(embed_docs, embed_targets, start),
        lambda: tuple(grads),
    )


def solution(mesh):
    axes = ROW + COL
    fine = jax.sharding.Mesh(mesh.devices.reshape([SIZES[a] for a in axes]), axes)
    return jax.shard_map(
        local,
        mesh=fine,
        in_specs=(P(ROW + COL, None), P(COL + ROW, None), P(COL)),
        out_specs=(P(ROW + COL, None), P(COL + ROW, None)),
        check_vma=False,
    )
```

```python
import math
from functools import partial

import jax
import jax.numpy as jnp
from jax import lax
from jax.experimental import pallas as pl
from jax.experimental.pallas import tpu as pltpu
from jax.sharding import PartitionSpec as P

smoothing_epsilon = 0.05
EXPONENT_MAX = 40.0
LOW, HIGH = 1e-25, 1e25
FIRST_LOW = 1e-9
KEPT, HELD = (0,), (0,)
ROW, COL = ("z_lo", "x", "core"), ("y", "z_hi")
SIZES = {"z_lo": 2, "x": 4, "core": 2, "y": 4, "z_hi": 4}


def row_log_mass(scores):
    largest = lax.pmax(jnp.max(scores, axis=1), COL)
    mass_all = lax.psum(jnp.sum(jnp.exp(scores - largest[:, None]), axis=1), COL)
    return largest + jnp.log(mass_all)


def column_log_mass(scores):
    largest = lax.pmax(jnp.max(scores, axis=0), ROW)
    mass_all = lax.psum(jnp.sum(jnp.exp(scores - largest[None, :]), axis=0), ROW)
    return largest + jnp.log(mass_all)


def log_domain(embed_docs, embed_targets, start):
    doc_block, target_block = gather(embed_docs, COL), gather(embed_targets, ROW)
    highest = lax.Precision.HIGHEST
    distance_tile = (
        jnp.sum(doc_block * doc_block, axis=1)[:, None]
        + jnp.sum(target_block * target_block, axis=1)[None, :]
        - 2.0 * jnp.dot(doc_block, target_block.T, precision=highest)
    )
    texts = distance_tile.shape[0] * lax.axis_size(ROW)
    goals = distance_tile.shape[1] * lax.axis_size(COL)
    ratio = texts / goals
    t = smoothing_epsilon
    row_log_one = row_log_mass((start[None, :] - distance_tile) / t)
    doc_one = t * math.log(goals) - t * row_log_one
    col_log_one = column_log_mass((doc_one[:, None] - distance_tile) / t)
    target_one = t * math.log(texts) - t * col_log_one
    row_log_two = row_log_mass((target_one[None, :] - distance_tile) / t)
    doc_two = t * math.log(goals) - t * row_log_two
    col_log_two = column_log_mass((doc_two[:, None] - distance_tile) / t)
    plan = jnp.exp((doc_two[:, None] - distance_tile) / t - col_log_two[None, :])
    adjoint = ratio * plan
    doc_bar_two = 1.0 - ratio * lax.psum(jnp.sum(plan, axis=1), COL)
    plan = jnp.exp((target_one[None, :] - distance_tile) / t - row_log_two[:, None])
    weighted = doc_bar_two[:, None] * plan
    adjoint = adjoint + weighted
    target_bar_one = -lax.psum(jnp.sum(weighted, axis=0), ROW)
    plan = jnp.exp((doc_one[:, None] - distance_tile) / t - col_log_one[None, :])
    weighted = target_bar_one[None, :] * plan
    adjoint = adjoint + weighted
    doc_bar_one = -lax.psum(jnp.sum(weighted, axis=1), COL)
    plan = jnp.exp((start[None, :] - distance_tile) / t - row_log_one[:, None])
    adjoint = adjoint + doc_bar_one[:, None] * plan
    doc_part = 2.0 * (
        jnp.sum(adjoint, axis=1)[:, None] * doc_block
        - jnp.dot(adjoint, target_block, precision=highest)
    )
    crossed = lax.dot_general(adjoint, doc_block, (((0,), (0,)), ((), ())), precision=highest)
    target_part = 2.0 * (jnp.sum(adjoint, axis=0)[:, None] * target_block - crossed)
    return scatter(doc_part, COL), scatter(target_part, ROW)


LANES = 128
f32, bf16 = jnp.float32, jnp.bfloat16


def swap(blocks, axis):
    return lax.all_to_all(blocks, axis, 0, 0)


def gather(block, axis):
    devices = lax.axis_size(axis)
    pieces = swap(jnp.broadcast_to(block[None], (devices, *block.shape)), axis)
    return pieces.reshape(devices * block.shape[0], *block.shape[1:])


def scatter(block, axis):
    devices = lax.axis_size(axis)
    pieces = block.reshape(devices, block.shape[0] // devices, *block.shape[1:])
    return jnp.sum(swap(pieces, axis), axis=0)


def inverse(mass, low, high):
    return jnp.where((mass >= low) & (mass <= high), 1.0 / mass, jnp.nan)


def halves(values):
    top = values.astype(bf16)
    return top, (values - top.astype(f32)).astype(bf16)


def spans(size, step):
    return [slice(i, i + step) for i in range(0, size, step)]


def upright(vector):
    return jnp.transpose(jnp.broadcast_to(vector, (LANES, LANES)))


def lane_total(block):
    return jnp.sum(jnp.transpose(block), axis=0, keepdims=True)


def row_sums(tile, weight):
    out = []
    for rows in spans(tile.shape[0], LANES):
        acc = None
        for c, cols in enumerate(spans(tile.shape[1], LANES)):
            term = tile[rows, cols] * weight[c : c + 1, :]
            acc = term if acc is None else acc + term
        out.append(lane_total(acc))
    return jnp.concatenate(out, axis=0)


def column_sums(tile, weight):
    columns = spans(tile.shape[1], LANES)
    acc = [None] * len(columns)
    for r, rows in enumerate(spans(tile.shape[0], LANES)):
        factor = upright(weight[r : r + 1, :])
        for c, cols in enumerate(columns):
            term = jnp.sum((tile[rows, cols] * factor).reshape(-1, 8, LANES), axis=0)
            acc[c] = term if acc[c] is None else acc[c] + term
    return jnp.concatenate([jnp.sum(a, axis=0, keepdims=True) for a in acc], axis=0)


def spread(ref, values):
    ref[...] = jnp.broadcast_to(values[None], ref.shape)


def turned(place, by, size):
    return lax.rem(place + by, size)


def kernel_tile(place, start, *refs):
    (ys, zs), (xs, ls) = (SIZES["y"], SIZES["z_hi"]), (SIZES["x"], SIZES["z_lo"])
    doc_pieces, mine, other = refs[:ys], refs[ys : ys + xs], refs[ys + xs : ys + 2 * xs]
    docs, targets, tile, weight_out, part, doc_wide, target_wide = refs[ys + 2 * xs :]
    features = docs.shape[1]
    share, target_share = docs.shape[0] // (ys * zs), targets.shape[0] // (2 * xs * ls)
    for k, source in enumerate(doc_pieces):
        for j in range(zs):
            at = (turned(place[0], ys - k, ys) * zs + turned(place[1], zs - j, zs)) * share
            docs[pl.ds(pl.multiple_of(at, share), share), :] = source[j * share : (j + 1) * share, :]
    for core, pieces in ((place[2], mine), (1 - place[2], other)):
        for k, source in enumerate(pieces):
            for j in range(ls):
                at = ((core * ls + turned(place[4], ls - j, ls)) * xs + turned(place[3], xs - k, xs)) * target_share
                targets[pl.ds(pl.multiple_of(at, target_share), target_share), :] = source[
                    j * target_share : (j + 1) * target_share, :
                ]
    for source, wide, order in ((docs, doc_wide, (0, 0, 1)), (targets, target_wide, (0, 1, 0))):
        for rows in spans(source.shape[0], 256):
            pair = halves(source[rows, :])
            for k, which in enumerate(order):
                wide[rows, k * features : (k + 1) * features] = pair[which]
    largest = None
    for cols in spans(targets.shape[0], 256):
        dots = lax.dot_general(
            doc_wide[...], target_wide[cols, :], (((1,), (1,)), ((), ())), preferred_element_type=f32
        )
        dots = dots * (2.0 / smoothing_epsilon)
        tile[:, cols] = jnp.exp(dots)
        peak = jnp.max(jnp.abs(dots).reshape(-1, 8, 256), axis=0)
        largest = peak if largest is None else jnp.maximum(largest, peak)
    fits = jnp.max(largest) <= EXPONENT_MAX
    norms = []
    for rows in spans(targets.shape[0], LANES):
        squares = targets[rows, :] * targets[rows, :]
        norms.append(lane_total(sum(squares[:, cols] for cols in spans(features, LANES))))
    count = start.shape[0]
    begin = jnp.concatenate([start[i : i + 1, :] for c in range(2) for i in range(c, count, 2)], axis=0)
    weight = jnp.exp((begin - jnp.concatenate(norms, axis=0)) / smoothing_epsilon)
    weight = jnp.where(fits, weight, jnp.nan)
    weight_out[...] = weight
    spread(part, row_sums(tile, weight))


def kernel_doc_one(tile, parts, weight_out, part):
    weight = inverse(jnp.sum(parts[...], axis=0), FIRST_LOW, HIGH)
    weight_out[...] = weight
    spread(part, column_sums(tile, weight))


def kernel_doc_two(tile, parts, weight_out, part):
    weight = inverse(jnp.sum(parts[...], axis=0), LOW, HIGH)
    weight_out[...] = weight
    spread(part, column_sums(tile, weight))


def kernel_target(tile, parts, weight_out, part):
    weight = inverse(jnp.sum(parts[...], axis=0), LOW, HIGH)
    weight_out[...] = weight
    spread(part, row_sums(tile, weight))


def kernel_bar_two(ratio, tile, parts, doc_two, weight_out, part):
    scale = doc_two[...]
    weight = scale * (1.0 - ratio * scale * jnp.sum(parts[...], axis=0))
    weight_out[...] = weight
    spread(part, column_sums(tile, weight))


def kernel_bar_one(tile, parts, target_one, weight_out, part):
    scale = target_one[...]
    weight = -scale * scale * jnp.sum(parts[...], axis=0)
    weight_out[...] = weight
    spread(part, row_sums(tile, weight))


def kernel_docs(ratio, place, tile, parts, doc_one, doc_two, bar_two, target_zero, target_one, target_two, bar_one,
                targets, top, low, mass, *refs):
    pieces, (factors, wide) = refs[:-2], refs[-2:]
    features = targets.shape[1]
    for rows in spans(targets.shape[0], 256):
        pair = halves(targets[rows, :])
        wide[rows, :features], wide[rows, features:] = pair
    one = doc_one[...]
    bar_zero = -one * one * jnp.sum(parts[...], axis=0)
    by_row = (bar_zero, ratio * doc_two[...], bar_two[...], one)
    by_column = (target_zero[...], target_two[...], target_one[...], bar_one[...])
    columns = spans(tile.shape[1], LANES)
    acc = [None] * len(columns)
    for r, rows in enumerate(spans(tile.shape[0], LANES)):
        for k, values in enumerate(by_row):
            factors[k, rows, :] = upright(values[r : r + 1, :])
    size = pieces[0].shape[0]
    for k, piece in enumerate(pieces):
        first = pl.multiple_of(turned(place[0], k, len(pieces)) * size, size)
        for rows in spans(size, 32):
            rows = pl.ds(first + rows.start, 32)
            a = [factors[i, rows, :] for i in range(4)]
            for c, cols in enumerate(columns):
                b = [v[c : c + 1, :] for v in by_column]
                adjoint = tile[rows, cols] * ((a[0] * b[0] + a[1] * b[1]) + (a[2] * b[2] + a[3] * b[3]))
                term = jnp.sum(adjoint.reshape(-1, 8, LANES), axis=0)
                acc[c] = term if acc[c] is None else acc[c] + term
                top[rows, cols], low[rows, cols] = halves(adjoint)
        block = pl.ds(first, size)
        both = jnp.dot(top[block, :], wide[...], preferred_element_type=f32)
        rest = jnp.dot(low[block, :], wide[:, :features], preferred_element_type=f32)
        piece[...] = (both[:, :features] + both[:, features:]) + rest
    mass[...] = jnp.concatenate([jnp.sum(a, axis=0, keepdims=True) for a in acc], axis=0)


def kernel_targets(place, top, low, mass, docs, targets, other, mine, flat):
    features = docs.shape[1]
    for rows in spans(docs.shape[0], 256):
        pair = halves(jnp.transpose(docs[rows, :]))
        flat[:features, rows], flat[features:, rows] = pair
    half = mine.shape[0]
    for core, out in ((1 - place[2], other), (place[2], mine)):
        for inner in spans(half, 256):
            first = pl.multiple_of(core * half + inner.start, 256)
            cols = pl.ds(first, 256)
            both = jnp.dot(flat[...], top[:, cols], preferred_element_type=f32)
            rest = jnp.dot(flat[:features, :], low[:, cols], preferred_element_type=f32)
            crossed = jnp.transpose((both[:features] + both[features:]) + rest)
            for rows in spans(256, LANES):
                at = core * (half // LANES) + (inner.start + rows.start) // LANES
                weight = upright(mass[pl.ds(at, 1), :])
                here = pl.ds(first + rows.start, LANES)
                for part in spans(features, LANES):
                    out[inner.start + rows.start : inner.start + rows.stop, part] = 2.0 * (
                        weight * targets[here, part] - crossed[rows, part]
                    )


def kernel_pieces(place, *refs):
    parts, pieces = refs[: SIZES["y"]], refs[SIZES["y"] :]
    size = pieces[0].shape[0]
    for k, piece in enumerate(pieces):
        rows = pl.ds(pl.multiple_of(turned(place[1], k, len(pieces)) * size, size), size)
        piece[...] = sum(part[rows, :] for part in parts)


def kernel_pair(one, two, out):
    out[...] = one[...] + two[...]


def kernel_grads(own, *refs):
    parts, (blocks, grad_docs, grad_targets) = refs[:-3], refs[-3:]
    grad_docs[...] = 2.0 * (own[...] - sum(part[...] for part in parts))
    grad_targets[...] = jnp.sum(blocks[...], axis=0)


def run(kernel, args, outs, scratch=(), limit=16, held=(), kept=(), flops=0, place=None):
    args = [pltpu.with_memory_space_constraint(a, pltpu.VMEM) if i in held else a for i, a in enumerate(args)]
    shapes = [pltpu.VMEM(*o) if i in kept else jax.ShapeDtypeStruct(*o) for i, o in enumerate(outs)]
    whole = pl.BlockSpec(memory_space=pltpu.VMEM)
    specs = [whole] * len(args)
    if place is not None:
        args, specs = [place, *args], [pl.BlockSpec(memory_space=pltpu.SMEM), *specs]
    size = sum(math.prod(a.shape) * a.dtype.itemsize for a in args)
    return pl.pallas_call(
        kernel,
        out_shape=shapes,
        in_specs=specs,
        out_specs=[whole] * len(outs),
        scratch_shapes=[pltpu.VMEM(*s) for s in scratch],
        compiler_params=pltpu.CompilerParams(vmem_limit_bytes=limit << 20),
        cost_estimate=pl.CostEstimate(flops=flops, bytes_accessed=size, transcendentals=0),
    )(*args)


def ring(blocks, axis):
    size = SIZES[axis]
    out = [blocks[0]] * size
    for k in sorted(range(1, size), key=lambda k: (min(k, size - k), k)):
        out[k] = lax.ppermute(blocks[k], axis, [(i, (i + k) % size) for i in range(size)])
    return out


def other_core(block):
    return lax.ppermute(block, "core", [(0, 1), (1, 0)])


def local(embed_docs, embed_targets, start):
    rows, cols = lax.axis_size(ROW), lax.axis_size(COL)
    place = jnp.stack([lax.axis_index(a) for a in ("y", "z_hi", "core", "x", "z_lo")]).astype(jnp.int32)
    near, beside = lax.optimization_barrier(
        (ring([embed_docs] * SIZES["z_hi"], "z_hi"), ring([embed_targets] * SIZES["z_lo"], "z_lo"))
    )
    mine = ring([jnp.concatenate(beside, axis=0)] * SIZES["x"], "x")
    doc_pieces = ring([jnp.concatenate(near, axis=0)] * SIZES["y"], "y")
    other = [other_core(block) for block in mine]
    doc_pieces, mine, other = lax.optimization_barrier((doc_pieces, mine, other))
    (share, features), (target_share, _) = embed_docs.shape, embed_targets.shape
    n, m = share * cols, target_share * rows
    ratio = (n * rows) / (m * cols)
    product = 6 * n * m * features
    doc_vector, target_vector = ((n // LANES, LANES), f32), ((m // LANES, LANES), f32)
    doc_parts, target_parts = ((cols, *doc_vector[0]), f32), ((rows, *target_vector[0]), f32)
    docs, targets, tile, target_zero, part = run(
        kernel_tile,
        (start.reshape(target_vector[0]), *doc_pieces, *mine, *other),
        [((n, features), f32), ((m, features), f32), ((n, m), f32), target_vector, doc_parts],
        [((n, 3 * features), bf16), ((m, 3 * features), bf16)],
        limit=28, kept=(2,), flops=product, place=place,
    )

    def step(kernel, part, axis, *extra, over_docs):
        outs = [doc_vector, target_parts] if over_docs else [target_vector, doc_parts]
        return run(kernel, (tile, swap(part, axis), *extra), outs, held=HELD, flops=2 * n * m)

    doc_one, part = step(kernel_doc_one, part, COL, over_docs=True)
    target_one, part = step(kernel_target, part, ROW, over_docs=False)
    doc_two, part = step(kernel_doc_two, part, COL, over_docs=True)
    target_two, part = step(kernel_target, part, ROW, over_docs=False)
    bar_two, part = step(partial(kernel_bar_two, ratio), part, COL, doc_two, over_docs=True)
    bar_one, part = step(kernel_bar_one, part, ROW, target_one, over_docs=False)
    top, low, mass, *doc_pieces = run(
        partial(kernel_docs, ratio),
        (tile, swap(part, COL), doc_one, doc_two, bar_two, target_zero, target_one, target_two, bar_one, targets),
        [((n, m), bf16), ((n, m), bf16), target_vector] + [((n // SIZES["y"], features), f32)] * SIZES["y"],
        [((4, n, LANES), f32), ((m, 2 * features), bf16)],
        limit=32, held=HELD, kept=(0, 1), flops=product, place=place,
    )
    doc_pieces = ring(doc_pieces, "y")
    other, mine = run(
        kernel_targets, (top, low, mass, docs, targets), [((m // 2, features), f32)] * 2, [((2 * features, n), bf16)],
        limit=24, held=(0, 1), flops=product, place=place,
    )
    (mine,) = run(kernel_pair, (mine, other_core(other)), [((m // 2, features), f32)])
    doc_pieces = run(kernel_pieces, doc_pieces, [((share, features), f32)] * SIZES["z_hi"], place=place)
    doc_pieces = ring(doc_pieces, "z_hi")
    blocks = swap(mine.reshape(rows // 2, target_share, features), ("z_lo", "x"))
    grads = run(
        kernel_grads, (embed_docs, *doc_pieces, blocks), [((share, features), f32), ((target_share, features), f32)]
    )
    return lax.cond(
        jnp.isnan(jnp.sum(bar_two)),
        lambda: log_domain(embed_docs, embed_targets, start),
        lambda: tuple(grads),
    )


def solution(mesh):
    axes = ROW + COL
    fine = jax.sharding.Mesh(mesh.devices.reshape([SIZES[a] for a in axes]), axes)
    return jax.shard_map(
        local,
        mesh=fine,
        in_specs=(P(ROW + COL, None), P(COL + ROW, None), P(COL)),
        out_specs=(P(ROW + COL, None), P(COL + ROW, None)),
        check_vma=False,
    )
```

```python
import math
from functools import partial

import jax
import jax.numpy as jnp
from jax import lax
from jax.experimental import pallas as pl
from jax.experimental.pallas import tpu as pltpu
from jax.sharding import PartitionSpec as P

smoothing_epsilon = 0.05
EXPONENT_MAX = 40.0
LOW, HIGH = 1e-25, 1e25
FIRST_LOW = 1e-9
KEPT, HELD = (0,), (0,)
ROW, COL = ("z_lo", "x", "core"), ("y", "z_hi")
SIZES = {"z_lo": 2, "x": 4, "core": 2, "y": 4, "z_hi": 4}


def row_log_mass(scores):
    largest = lax.pmax(jnp.max(scores, axis=1), COL)
    mass_all = lax.psum(jnp.sum(jnp.exp(scores - largest[:, None]), axis=1), COL)
    return largest + jnp.log(mass_all)


def column_log_mass(scores):
    largest = lax.pmax(jnp.max(scores, axis=0), ROW)
    mass_all = lax.psum(jnp.sum(jnp.exp(scores - largest[None, :]), axis=0), ROW)
    return largest + jnp.log(mass_all)


def log_domain(embed_docs, embed_targets, start):
    doc_block, target_block = gather(embed_docs, COL), gather(embed_targets, ROW)
    highest = lax.Precision.HIGHEST
    distance_tile = (
        jnp.sum(doc_block * doc_block, axis=1)[:, None]
        + jnp.sum(target_block * target_block, axis=1)[None, :]
        - 2.0 * jnp.dot(doc_block, target_block.T, precision=highest)
    )
    texts = distance_tile.shape[0] * lax.axis_size(ROW)
    goals = distance_tile.shape[1] * lax.axis_size(COL)
    ratio = texts / goals
    t = smoothing_epsilon
    row_log_one = row_log_mass((start[None, :] - distance_tile) / t)
    doc_one = t * math.log(goals) - t * row_log_one
    col_log_one = column_log_mass((doc_one[:, None] - distance_tile) / t)
    target_one = t * math.log(texts) - t * col_log_one
    row_log_two = row_log_mass((target_one[None, :] - distance_tile) / t)
    doc_two = t * math.log(goals) - t * row_log_two
    col_log_two = column_log_mass((doc_two[:, None] - distance_tile) / t)
    plan = jnp.exp((doc_two[:, None] - distance_tile) / t - col_log_two[None, :])
    adjoint = ratio * plan
    doc_bar_two = 1.0 - ratio * lax.psum(jnp.sum(plan, axis=1), COL)
    plan = jnp.exp((target_one[None, :] - distance_tile) / t - row_log_two[:, None])
    weighted = doc_bar_two[:, None] * plan
    adjoint = adjoint + weighted
    target_bar_one = -lax.psum(jnp.sum(weighted, axis=0), ROW)
    plan = jnp.exp((doc_one[:, None] - distance_tile) / t - col_log_one[None, :])
    weighted = target_bar_one[None, :] * plan
    adjoint = adjoint + weighted
    doc_bar_one = -lax.psum(jnp.sum(weighted, axis=1), COL)
    plan = jnp.exp((start[None, :] - distance_tile) / t - row_log_one[:, None])
    adjoint = adjoint + doc_bar_one[:, None] * plan
    doc_part = 2.0 * (
        jnp.sum(adjoint, axis=1)[:, None] * doc_block
        - jnp.dot(adjoint, target_block, precision=highest)
    )
    crossed = lax.dot_general(adjoint, doc_block, (((0,), (0,)), ((), ())), precision=highest)
    target_part = 2.0 * (jnp.sum(adjoint, axis=0)[:, None] * target_block - crossed)
    return scatter(doc_part, COL), scatter(target_part, ROW)


LANES = 128
f32, bf16 = jnp.float32, jnp.bfloat16


def swap(blocks, axis):
    return lax.all_to_all(blocks, axis, 0, 0)


def gather(block, axis):
    devices = lax.axis_size(axis)
    pieces = swap(jnp.broadcast_to(block[None], (devices, *block.shape)), axis)
    return pieces.reshape(devices * block.shape[0], *block.shape[1:])


def scatter(block, axis):
    devices = lax.axis_size(axis)
    pieces = block.reshape(devices, block.shape[0] // devices, *block.shape[1:])
    return jnp.sum(swap(pieces, axis), axis=0)


def inverse(mass, low, high):
    return jnp.where((mass >= low) & (mass <= high), 1.0 / mass, jnp.nan)


def halves(values):
    top = values.astype(bf16)
    return top, (values - top.astype(f32)).astype(bf16)


def spans(size, step):
    return [slice(i, i + step) for i in range(0, size, step)]


def upright(vector):
    return jnp.transpose(jnp.broadcast_to(vector, (LANES, LANES)))


def lane_total(block):
    return jnp.sum(jnp.transpose(block), axis=0, keepdims=True)


def row_sums(tile, weight):
    out = []
    for rows in spans(tile.shape[0], LANES):
        acc = None
        for c, cols in enumerate(spans(tile.shape[1], LANES)):
            term = tile[rows, cols] * weight[c : c + 1, :]
            acc = term if acc is None else acc + term
        out.append(lane_total(acc))
    return jnp.concatenate(out, axis=0)


def column_sums(tile, weight):
    columns = spans(tile.shape[1], LANES)
    acc = [None] * len(columns)
    for r, rows in enumerate(spans(tile.shape[0], LANES)):
        factor = upright(weight[r : r + 1, :])
        for c, cols in enumerate(columns):
            term = jnp.sum((tile[rows, cols] * factor).reshape(-1, 8, LANES), axis=0)
            acc[c] = term if acc[c] is None else acc[c] + term
    return jnp.concatenate([jnp.sum(a, axis=0, keepdims=True) for a in acc], axis=0)


def spread(ref, values):
    ref[...] = jnp.broadcast_to(values[None], ref.shape)


def turned(place, by, size):
    return lax.rem(place + by, size)


def kernel_tile(place, start, *refs):
    (ys, zs), (xs, ls) = (SIZES["y"], SIZES["z_hi"]), (SIZES["x"], SIZES["z_lo"])
    doc_pieces, mine, other = refs[:ys], refs[ys : ys + xs], refs[ys + xs : ys + 2 * xs]
    docs, targets, tile, weight_out, part, doc_wide, target_wide = refs[ys + 2 * xs :]
    features = docs.shape[1]
    share, target_share = docs.shape[0] // (ys * zs), targets.shape[0] // (2 * xs * ls)
    for k, source in enumerate(doc_pieces):
        for j in range(zs):
            at = (turned(place[0], ys - k, ys) * zs + turned(place[1], zs - j, zs)) * share
            docs[pl.ds(pl.multiple_of(at, share), share), :] = source[j * share : (j + 1) * share, :]
    for core, pieces in ((place[2], mine), (1 - place[2], other)):
        for k, source in enumerate(pieces):
            for j in range(ls):
                at = ((core * ls + turned(place[4], ls - j, ls)) * xs + turned(place[3], xs - k, xs)) * target_share
                targets[pl.ds(pl.multiple_of(at, target_share), target_share), :] = source[
                    j * target_share : (j + 1) * target_share, :
                ]
    for source, wide, order in ((docs, doc_wide, (0, 0, 1)), (targets, target_wide, (0, 1, 0))):
        for rows in spans(source.shape[0], 256):
            pair = halves(source[rows, :])
            for k, which in enumerate(order):
                wide[rows, k * features : (k + 1) * features] = pair[which]
    largest = None
    for cols in spans(targets.shape[0], 256):
        dots = lax.dot_general(
            doc_wide[...], target_wide[cols, :], (((1,), (1,)), ((), ())), preferred_element_type=f32
        )
        dots = dots * (2.0 / smoothing_epsilon)
        tile[:, cols] = jnp.exp(dots)
        peak = jnp.max(jnp.abs(dots).reshape(-1, 8, 256), axis=0)
        largest = peak if largest is None else jnp.maximum(largest, peak)
    fits = jnp.max(largest) <= EXPONENT_MAX
    norms = []
    for rows in spans(targets.shape[0], LANES):
        squares = targets[rows, :] * targets[rows, :]
        norms.append(lane_total(sum(squares[:, cols] for cols in spans(features, LANES))))
    count = start.shape[0]
    begin = jnp.concatenate([start[i : i + 1, :] for c in range(2) for i in range(c, count, 2)], axis=0)
    weight = jnp.exp((begin - jnp.concatenate(norms, axis=0)) / smoothing_epsilon)
    weight = jnp.where(fits, weight, jnp.nan)
    weight_out[...] = weight
    spread(part, row_sums(tile, weight))


def kernel_doc_one(tile, parts, weight_out, part):
    weight = inverse(jnp.sum(parts[...], axis=0), FIRST_LOW, HIGH)
    weight_out[...] = weight
    spread(part, column_sums(tile, weight))


def kernel_doc_two(tile, parts, weight_out, part):
    weight = inverse(jnp.sum(parts[...], axis=0), LOW, HIGH)
    weight_out[...] = weight
    spread(part, column_sums(tile, weight))


def kernel_target(tile, parts, weight_out, part):
    weight = inverse(jnp.sum(parts[...], axis=0), LOW, HIGH)
    weight_out[...] = weight
    spread(part, row_sums(tile, weight))


def kernel_bar_two(ratio, tile, parts, doc_two, weight_out, part):
    scale = doc_two[...]
    weight = scale * (1.0 - ratio * scale * jnp.sum(parts[...], axis=0))
    weight_out[...] = weight
    spread(part, column_sums(tile, weight))


def kernel_bar_one(tile, parts, target_one, weight_out, part):
    scale = target_one[...]
    weight = -scale * scale * jnp.sum(parts[...], axis=0)
    weight_out[...] = weight
    spread(part, row_sums(tile, weight))


def kernel_docs(ratio, place, tile, parts, doc_one, doc_two, bar_two, target_zero, target_one, target_two, bar_one,
                targets, top, low, mass, *refs):
    pieces, (factors, wide) = refs[:-2], refs[-2:]
    features = targets.shape[1]
    for rows in spans(targets.shape[0], 256):
        pair = halves(targets[rows, :])
        wide[rows, :features], wide[rows, features:] = pair
    one = doc_one[...]
    bar_zero = -one * one * jnp.sum(parts[...], axis=0)
    by_row = (bar_zero, ratio * doc_two[...], bar_two[...], one)
    by_column = (target_zero[...], target_two[...], target_one[...], bar_one[...])
    columns = spans(tile.shape[1], LANES)
    acc = [None] * len(columns)
    for r, rows in enumerate(spans(tile.shape[0], LANES)):
        for k, values in enumerate(by_row):
            factors[k, rows, :] = upright(values[r : r + 1, :])
    size = pieces[0].shape[0]
    for k, piece in enumerate(pieces):
        first = pl.multiple_of(turned(place[0], k, len(pieces)) * size, size)
        for rows in spans(size, 32):
            rows = pl.ds(first + rows.start, 32)
            a = [factors[i, rows, :] for i in range(4)]
            for c, cols in enumerate(columns):
                b = [v[c : c + 1, :] for v in by_column]
                adjoint = tile[rows, cols] * ((a[0] * b[0] + a[1] * b[1]) + (a[2] * b[2] + a[3] * b[3]))
                term = jnp.sum(adjoint.reshape(-1, 8, LANES), axis=0)
                acc[c] = term if acc[c] is None else acc[c] + term
                top[rows, cols], low[rows, cols] = halves(adjoint)
        block = pl.ds(first, size)
        both = jnp.dot(top[block, :], wide[...], preferred_element_type=f32)
        rest = jnp.dot(low[block, :], wide[:, :features], preferred_element_type=f32)
        piece[...] = (both[:, :features] + both[:, features:]) + rest
    mass[...] = jnp.concatenate([jnp.sum(a, axis=0, keepdims=True) for a in acc], axis=0)


def kernel_targets(place, top, low, mass, docs, targets, other, mine, flat):
    features = docs.shape[1]
    for rows in spans(docs.shape[0], 256):
        pair = halves(jnp.transpose(docs[rows, :]))
        flat[:features, rows], flat[features:, rows] = pair
    half = mine.shape[0]
    for core, out in ((1 - place[2], other), (place[2], mine)):
        for inner in spans(half, 256):
            first = pl.multiple_of(core * half + inner.start, 256)
            cols = pl.ds(first, 256)
            both = jnp.dot(flat[...], top[:, cols], preferred_element_type=f32)
            rest = jnp.dot(flat[:features, :], low[:, cols], preferred_element_type=f32)
            crossed = jnp.transpose((both[:features] + both[features:]) + rest)
            for rows in spans(256, LANES):
                at = core * (half // LANES) + (inner.start + rows.start) // LANES
                weight = upright(mass[pl.ds(at, 1), :])
                here = pl.ds(first + rows.start, LANES)
                for part in spans(features, LANES):
                    out[inner.start + rows.start : inner.start + rows.stop, part] = 2.0 * (
                        weight * targets[here, part] - crossed[rows, part]
                    )


def kernel_pieces(place, *refs):
    parts, pieces = refs[: SIZES["y"]], refs[SIZES["y"] :]
    size = pieces[0].shape[0]
    for k, piece in enumerate(pieces):
        rows = pl.ds(pl.multiple_of(turned(place[1], k, len(pieces)) * size, size), size)
        piece[...] = sum(part[rows, :] for part in parts)


def kernel_pair(one, two, out):
    out[...] = one[...] + two[...]


def kernel_grads(own, *refs):
    parts, (blocks, grad_docs, grad_targets) = refs[:-3], refs[-3:]
    grad_docs[...] = 2.0 * (own[...] - sum(part[...] for part in parts))
    grad_targets[...] = jnp.sum(blocks[...], axis=0)


def run(kernel, args, outs, scratch=(), limit=16, held=(), kept=(), flops=0, place=None):
    args = [pltpu.with_memory_space_constraint(a, pltpu.VMEM) if i in held else a for i, a in enumerate(args)]
    shapes = [pltpu.VMEM(*o) if i in kept else jax.ShapeDtypeStruct(*o) for i, o in enumerate(outs)]
    whole = pl.BlockSpec(memory_space=pltpu.VMEM)
    specs = [whole] * len(args)
    if place is not None:
        args, specs = [place, *args], [pl.BlockSpec(memory_space=pltpu.SMEM), *specs]
    size = sum(math.prod(a.shape) * a.dtype.itemsize for a in args)
    return pl.pallas_call(
        kernel,
        out_shape=shapes,
        in_specs=specs,
        out_specs=[whole] * len(outs),
        scratch_shapes=[pltpu.VMEM(*s) for s in scratch],
        compiler_params=pltpu.CompilerParams(vmem_limit_bytes=limit << 20),
        cost_estimate=pl.CostEstimate(flops=flops, bytes_accessed=size, transcendentals=0),
    )(*args)


def ring(blocks, axis):
    size = SIZES[axis]
    out = [blocks[0]] * size
    for k in sorted(range(1, size), key=lambda k: (min(k, size - k), k)):
        out[k] = lax.ppermute(blocks[k], axis, [(i, (i + k) % size) for i in range(size)])
    return out


def other_core(block):
    return lax.ppermute(block, "core", [(0, 1), (1, 0)])


def local(embed_docs, embed_targets, start):
    rows, cols = lax.axis_size(ROW), lax.axis_size(COL)
    place = jnp.stack([lax.axis_index(a) for a in ("y", "z_hi", "core", "x", "z_lo")]).astype(jnp.int32)
    near, beside = lax.optimization_barrier(
        (ring([embed_docs] * SIZES["z_hi"], "z_hi"), ring([embed_targets] * SIZES["z_lo"], "z_lo"))
    )
    mine = ring([jnp.concatenate(beside, axis=0)] * SIZES["x"], "x")
    doc_pieces = ring([jnp.concatenate(near, axis=0)] * SIZES["y"], "y")
    other = [other_core(block) for block in mine]
    doc_pieces, mine, other = lax.optimization_barrier((doc_pieces, mine, other))
    (share, features), (target_share, _) = embed_docs.shape, embed_targets.shape
    n, m = share * cols, target_share * rows
    ratio = (n * rows) / (m * cols)
    product = 6 * n * m * features
    doc_vector, target_vector = ((n // LANES, LANES), f32), ((m // LANES, LANES), f32)
    doc_parts, target_parts = ((cols, *doc_vector[0]), f32), ((rows, *target_vector[0]), f32)
    docs, targets, tile, target_zero, part = run(
        kernel_tile,
        (start.reshape(target_vector[0]), *doc_pieces, *mine, *other),
        [((n, features), f32), ((m, features), f32), ((n, m), f32), target_vector, doc_parts],
        [((n, 3 * features), bf16), ((m, 3 * features), bf16)],
        limit=28, kept=(2,), flops=product, place=place,
    )

    def step(kernel, part, axis, *extra, over_docs):
        outs = [doc_vector, target_parts] if over_docs else [target_vector, doc_parts]
        return run(kernel, (tile, swap(part, axis), *extra), outs, held=HELD, flops=2 * n * m)

    doc_one, part = step(kernel_doc_one, part, COL, over_docs=True)
    target_one, part = step(kernel_target, part, ROW, over_docs=False)
    doc_two, part = step(kernel_doc_two, part, COL, over_docs=True)
    target_two, part = step(kernel_target, part, ROW, over_docs=False)
    bar_two, part = step(partial(kernel_bar_two, ratio), part, COL, doc_two, over_docs=True)
    bar_one, part = step(kernel_bar_one, part, ROW, target_one, over_docs=False)
    top, low, mass, *doc_pieces = run(
        partial(kernel_docs, ratio),
        (tile, swap(part, COL), doc_one, doc_two, bar_two, target_zero, target_one, target_two, bar_one, targets),
        [((n, m), bf16), ((n, m), bf16), target_vector] + [((n // SIZES["y"], features), f32)] * SIZES["y"],
        [((4, n, LANES), f32), ((m, 2 * features), bf16)],
        limit=32, held=HELD, kept=(0, 1), flops=product, place=place,
    )
    doc_pieces = ring(doc_pieces, "y")
    other, mine = run(
        kernel_targets, (top, low, mass, docs, targets), [((m // 2, features), f32)] * 2, [((2 * features, n), bf16)],
        limit=24, held=(0, 1), flops=product, place=place,
    )
    (mine,) = run(kernel_pair, (mine, other_core(other)), [((m // 2, features), f32)])
    doc_pieces = run(kernel_pieces, doc_pieces, [((share, features), f32)] * SIZES["z_hi"], place=place)
    doc_pieces = ring(doc_pieces, "z_hi")
    blocks = swap(mine.reshape(rows // 2, target_share, features), ("z_lo", "x"))
    grads = run(
        kernel_grads, (embed_docs, *doc_pieces, blocks), [((share, features), f32), ((target_share, features), f32)]
    )
    return lax.while_loop(
        lambda state: state[0],
        lambda state: (False, *log_domain(embed_docs, embed_targets, start)),
        (jnp.isnan(jnp.sum(bar_two)), *grads),
    )[1:]


def solution(mesh):
    axes = ROW + COL
    fine = jax.sharding.Mesh(mesh.devices.reshape([SIZES[a] for a in axes]), axes)
    return jax.shard_map(
        local,
        mesh=fine,
        in_specs=(P(ROW + COL, None), P(COL + ROW, None), P(COL)),
        out_specs=(P(ROW + COL, None), P(COL + ROW, None)),
        check_vma=False,
    )
```

```python
import math
from functools import partial

import jax
import jax.numpy as jnp
from jax import lax
from jax.experimental import pallas as pl
from jax.experimental.pallas import tpu as pltpu
from jax.sharding import PartitionSpec as P

smoothing_epsilon = 0.05
EXPONENT_MAX = 40.0
LOW, HIGH = 1e-25, 1e25
FIRST_LOW = 1e-9
KEPT, HELD = (0,), (0,)
ROW, COL = ("z_lo", "x", "core"), ("y", "z_hi")
SIZES = {"z_lo": 2, "x": 4, "core": 2, "y": 4, "z_hi": 4}


def row_log_mass(scores):
    largest = lax.pmax(jnp.max(scores, axis=1), COL)
    mass_all = lax.psum(jnp.sum(jnp.exp(scores - largest[:, None]), axis=1), COL)
    return largest + jnp.log(mass_all)


def column_log_mass(scores):
    largest = lax.pmax(jnp.max(scores, axis=0), ROW)
    mass_all = lax.psum(jnp.sum(jnp.exp(scores - largest[None, :]), axis=0), ROW)
    return largest + jnp.log(mass_all)


def log_domain(embed_docs, embed_targets, start):
    doc_block, target_block = gather(embed_docs, COL), gather(embed_targets, ROW)
    highest = lax.Precision.HIGHEST
    distance_tile = (
        jnp.sum(doc_block * doc_block, axis=1)[:, None]
        + jnp.sum(target_block * target_block, axis=1)[None, :]
        - 2.0 * jnp.dot(doc_block, target_block.T, precision=highest)
    )
    texts = distance_tile.shape[0] * lax.axis_size(ROW)
    goals = distance_tile.shape[1] * lax.axis_size(COL)
    ratio = texts / goals
    t = smoothing_epsilon
    row_log_one = row_log_mass((start[None, :] - distance_tile) / t)
    doc_one = t * math.log(goals) - t * row_log_one
    col_log_one = column_log_mass((doc_one[:, None] - distance_tile) / t)
    target_one = t * math.log(texts) - t * col_log_one
    row_log_two = row_log_mass((target_one[None, :] - distance_tile) / t)
    doc_two = t * math.log(goals) - t * row_log_two
    col_log_two = column_log_mass((doc_two[:, None] - distance_tile) / t)
    plan = jnp.exp((doc_two[:, None] - distance_tile) / t - col_log_two[None, :])
    adjoint = ratio * plan
    doc_bar_two = 1.0 - ratio * lax.psum(jnp.sum(plan, axis=1), COL)
    plan = jnp.exp((target_one[None, :] - distance_tile) / t - row_log_two[:, None])
    weighted = doc_bar_two[:, None] * plan
    adjoint = adjoint + weighted
    target_bar_one = -lax.psum(jnp.sum(weighted, axis=0), ROW)
    plan = jnp.exp((doc_one[:, None] - distance_tile) / t - col_log_one[None, :])
    weighted = target_bar_one[None, :] * plan
    adjoint = adjoint + weighted
    doc_bar_one = -lax.psum(jnp.sum(weighted, axis=1), COL)
    plan = jnp.exp((start[None, :] - distance_tile) / t - row_log_one[:, None])
    adjoint = adjoint + doc_bar_one[:, None] * plan
    doc_part = 2.0 * (
        jnp.sum(adjoint, axis=1)[:, None] * doc_block
        - jnp.dot(adjoint, target_block, precision=highest)
    )
    crossed = lax.dot_general(adjoint, doc_block, (((0,), (0,)), ((), ())), precision=highest)
    target_part = 2.0 * (jnp.sum(adjoint, axis=0)[:, None] * target_block - crossed)
    return scatter(doc_part, COL), scatter(target_part, ROW)


LANES = 128
f32, bf16 = jnp.float32, jnp.bfloat16


def swap(blocks, axis):
    return lax.all_to_all(blocks, axis, 0, 0)


def gather(block, axis):
    devices = lax.axis_size(axis)
    pieces = swap(jnp.broadcast_to(block[None], (devices, *block.shape)), axis)
    return pieces.reshape(devices * block.shape[0], *block.shape[1:])


def scatter(block, axis):
    devices = lax.axis_size(axis)
    pieces = block.reshape(devices, block.shape[0] // devices, *block.shape[1:])
    return jnp.sum(swap(pieces, axis), axis=0)


def inverse(mass, low, high):
    return jnp.where((mass >= low) & (mass <= high), 1.0 / mass, jnp.nan)


def halves(values):
    top = values.astype(bf16)
    return top, (values - top.astype(f32)).astype(bf16)


def spans(size, step):
    return [slice(i, i + step) for i in range(0, size, step)]


def upright(vector):
    return jnp.transpose(jnp.broadcast_to(vector, (LANES, LANES)))


def lane_total(block):
    return jnp.sum(jnp.transpose(block), axis=0, keepdims=True)


def row_sums(tile, weight):
    out = []
    for rows in spans(tile.shape[0], LANES):
        acc = None
        for c, cols in enumerate(spans(tile.shape[1], LANES)):
            term = tile[rows, cols] * weight[c : c + 1, :]
            acc = term if acc is None else acc + term
        out.append(lane_total(acc))
    return jnp.concatenate(out, axis=0)


def column_sums(tile, weight):
    columns = spans(tile.shape[1], LANES)
    acc = [None] * len(columns)
    for r, rows in enumerate(spans(tile.shape[0], LANES)):
        factor = upright(weight[r : r + 1, :])
        for c, cols in enumerate(columns):
            term = jnp.sum((tile[rows, cols] * factor).reshape(-1, 8, LANES), axis=0)
            acc[c] = term if acc[c] is None else acc[c] + term
    return jnp.concatenate([jnp.sum(a, axis=0, keepdims=True) for a in acc], axis=0)


def spread(ref, values):
    ref[...] = jnp.broadcast_to(values[None], ref.shape)


def turned(place, by, size):
    return lax.rem(place + by, size)


def kernel_tile(place, start, *refs):
    (ys, zs), (xs, ls) = (SIZES["y"], SIZES["z_hi"]), (SIZES["x"], SIZES["z_lo"])
    doc_pieces, mine, other = refs[:ys], refs[ys : ys + xs], refs[ys + xs : ys + 2 * xs]
    docs, targets, tile, weight_out, part, doc_wide, target_wide = refs[ys + 2 * xs :]
    features = docs.shape[1]
    share, target_share = docs.shape[0] // (ys * zs), targets.shape[0] // (2 * xs * ls)
    for k, source in enumerate(doc_pieces):
        for j in range(zs):
            at = (turned(place[0], ys - k, ys) * zs + turned(place[1], zs - j, zs)) * share
            docs[pl.ds(pl.multiple_of(at, share), share), :] = source[j * share : (j + 1) * share, :]
    for core, pieces in ((place[2], mine), (1 - place[2], other)):
        for k, source in enumerate(pieces):
            for j in range(ls):
                at = ((core * ls + turned(place[4], ls - j, ls)) * xs + turned(place[3], xs - k, xs)) * target_share
                targets[pl.ds(pl.multiple_of(at, target_share), target_share), :] = source[
                    j * target_share : (j + 1) * target_share, :
                ]
    for source, wide, order in ((docs, doc_wide, (0, 0, 1)), (targets, target_wide, (0, 1, 0))):
        for rows in spans(source.shape[0], 256):
            pair = halves(source[rows, :])
            for k, which in enumerate(order):
                wide[rows, k * features : (k + 1) * features] = pair[which]
    norms = []
    for rows in spans(targets.shape[0], LANES):
        squares = targets[rows, :] * targets[rows, :]
        norms.append(lane_total(sum(squares[:, cols] for cols in spans(features, LANES))))
    count = start.shape[0]
    begin = jnp.concatenate([start[i : i + 1, :] for c in range(2) for i in range(c, count, 2)], axis=0)
    weight = jnp.exp((begin - jnp.concatenate(norms, axis=0)) / smoothing_epsilon)
    largest = None
    for c, cols in enumerate(spans(targets.shape[0], 256)):
        dots = lax.dot_general(
            doc_wide[...], target_wide[cols, :], (((1,), (1,)), ((), ())), preferred_element_type=f32
        )
        dots = dots * (2.0 / smoothing_epsilon)
        masses = jnp.exp(dots)
        tile[:, cols] = masses
        peak = jnp.max(jnp.abs(dots).reshape(-1, 8, 256), axis=0)
        largest = peak if largest is None else jnp.maximum(largest, peak)
    fits = jnp.max(largest) <= EXPONENT_MAX
    weight = jnp.where(fits, weight, jnp.nan)
    weight_out[...] = weight
    spread(part, row_sums(tile, weight))


def kernel_doc_one(tile, parts, weight_out, part):
    weight = inverse(jnp.sum(parts[...], axis=0), FIRST_LOW, HIGH)
    weight_out[...] = weight
    spread(part, column_sums(tile, weight))


def kernel_doc_two(tile, parts, weight_out, part):
    weight = inverse(jnp.sum(parts[...], axis=0), LOW, HIGH)
    weight_out[...] = weight
    spread(part, column_sums(tile, weight))


def kernel_target(tile, parts, weight_out, part):
    weight = inverse(jnp.sum(parts[...], axis=0), LOW, HIGH)
    weight_out[...] = weight
    spread(part, row_sums(tile, weight))


def kernel_bar_two(ratio, tile, parts, doc_two, weight_out, part):
    scale = doc_two[...]
    weight = scale * (1.0 - ratio * scale * jnp.sum(parts[...], axis=0))
    weight_out[...] = weight
    spread(part, column_sums(tile, weight))


def kernel_bar_one(tile, parts, target_one, weight_out, part):
    scale = target_one[...]
    weight = -scale * scale * jnp.sum(parts[...], axis=0)
    weight_out[...] = weight
    spread(part, row_sums(tile, weight))


def kernel_docs(ratio, place, tile, parts, doc_one, doc_two, bar_two, target_zero, target_one, target_two, bar_one,
                targets, top, low, mass, *refs):
    pieces, (factors, wide, sums) = refs[:-3], refs[-3:]
    features = targets.shape[1]
    for rows in spans(targets.shape[0], 256):
        pair = halves(targets[rows, :])
        wide[rows, :features], wide[rows, features:] = pair
    one = doc_one[...]
    bar_zero = -one * one * jnp.sum(parts[...], axis=0)
    by_row = (bar_zero, ratio * doc_two[...], bar_two[...], one)
    by_column = (target_zero[...], target_two[...], target_one[...], bar_one[...])
    columns = spans(tile.shape[1], LANES)
    acc = [None] * len(columns)
    for r, rows in enumerate(spans(tile.shape[0], LANES)):
        for k, values in enumerate(by_row):
            factors[k, rows, :] = upright(values[r : r + 1, :])

    def form(rows):
        a = [factors[i, rows, :] for i in range(4)]
        for c, cols in enumerate(columns):
            b = [v[c : c + 1, :] for v in by_column]
            adjoint = tile[rows, cols] * ((a[0] * b[0] + a[1] * b[1]) + (a[2] * b[2] + a[3] * b[3]))
            term = jnp.sum(adjoint.reshape(-1, 8, LANES), axis=0)
            acc[c] = term if acc[c] is None else acc[c] + term
            top[rows, cols], low[rows, cols] = halves(adjoint)

    def multiply(block):
        both = jnp.dot(top[block, :], wide[...], preferred_element_type=f32)
        rest = jnp.dot(low[block, :], wide[:, :features], preferred_element_type=f32)
        sums[block, :] = (both[:, :features] + both[:, features:]) + rest

    size = pieces[0].shape[0]
    for block in spans(tile.shape[0], 256):
        for rows in spans(256, 32):
            form(slice(block.start + rows.start, block.start + rows.stop))
        multiply(block)
    for k, piece in enumerate(pieces):
        piece[...] = sums[pl.ds(pl.multiple_of(turned(place[0], k, len(pieces)) * size, size), size), :]
    mass[...] = jnp.concatenate([jnp.sum(a, axis=0, keepdims=True) for a in acc], axis=0)


def kernel_targets(place, top, low, mass, docs, targets, other, mine, flat):
    features = docs.shape[1]
    for rows in spans(docs.shape[0], 256):
        pair = halves(jnp.transpose(docs[rows, :]))
        flat[:features, rows], flat[features:, rows] = pair
    half = mine.shape[0]
    for core, out in ((1 - place[2], other), (place[2], mine)):
        for inner in spans(half, 256):
            first = pl.multiple_of(core * half + inner.start, 256)
            cols = pl.ds(first, 256)
            both = jnp.dot(flat[...], top[:, cols], preferred_element_type=f32)
            rest = jnp.dot(flat[:features, :], low[:, cols], preferred_element_type=f32)
            crossed = jnp.transpose((both[:features] + both[features:]) + rest)
            for rows in spans(256, LANES):
                at = core * (half // LANES) + (inner.start + rows.start) // LANES
                weight = upright(mass[pl.ds(at, 1), :])
                here = pl.ds(first + rows.start, LANES)
                for part in spans(features, LANES):
                    out[inner.start + rows.start : inner.start + rows.stop, part] = 2.0 * (
                        weight * targets[here, part] - crossed[rows, part]
                    )


def kernel_pieces(place, *refs):
    parts, pieces = refs[: SIZES["y"]], refs[SIZES["y"] :]
    size = pieces[0].shape[0]
    for k, piece in enumerate(pieces):
        rows = pl.ds(pl.multiple_of(turned(place[1], k, len(pieces)) * size, size), size)
        piece[...] = sum(part[rows, :] for part in parts)


def kernel_pair(one, two, out):
    out[...] = one[...] + two[...]


def kernel_grads(own, *refs):
    parts, (blocks, grad_docs, grad_targets) = refs[:-3], refs[-3:]
    grad_docs[...] = 2.0 * (own[...] - sum(part[...] for part in parts))
    grad_targets[...] = jnp.sum(blocks[...], axis=0)


def run(kernel, args, outs, scratch=(), limit=16, held=(), kept=(), flops=0, place=None):
    args = [pltpu.with_memory_space_constraint(a, pltpu.VMEM) if i in held else a for i, a in enumerate(args)]
    shapes = [pltpu.VMEM(*o) if i in kept else jax.ShapeDtypeStruct(*o) for i, o in enumerate(outs)]
    whole = pl.BlockSpec(memory_space=pltpu.VMEM)
    specs = [whole] * len(args)
    if place is not None:
        args, specs = [place, *args], [pl.BlockSpec(memory_space=pltpu.SMEM), *specs]
    size = sum(math.prod(a.shape) * a.dtype.itemsize for a in args)
    return pl.pallas_call(
        kernel,
        out_shape=shapes,
        in_specs=specs,
        out_specs=[whole] * len(outs),
        scratch_shapes=[pltpu.VMEM(*s) for s in scratch],
        compiler_params=pltpu.CompilerParams(vmem_limit_bytes=limit << 20),
        cost_estimate=pl.CostEstimate(flops=flops, bytes_accessed=size, transcendentals=0),
    )(*args)


def ring(blocks, axis):
    size = SIZES[axis]
    out = [blocks[0]] * size
    for k in sorted(range(1, size), key=lambda k: (min(k, size - k), k)):
        out[k] = lax.ppermute(blocks[k], axis, [(i, (i + k) % size) for i in range(size)])
    return out


def other_core(block):
    return lax.ppermute(block, "core", [(0, 1), (1, 0)])


def local(embed_docs, embed_targets, start):
    rows, cols = lax.axis_size(ROW), lax.axis_size(COL)
    place = jnp.stack([lax.axis_index(a) for a in ("y", "z_hi", "core", "x", "z_lo")]).astype(jnp.int32)
    near, beside = lax.optimization_barrier(
        (ring([embed_docs] * SIZES["z_hi"], "z_hi"), ring([embed_targets] * SIZES["z_lo"], "z_lo"))
    )
    mine = ring([jnp.concatenate(beside, axis=0)] * SIZES["x"], "x")
    doc_pieces = ring([jnp.concatenate(near, axis=0)] * SIZES["y"], "y")
    other = [other_core(block) for block in mine]
    doc_pieces, mine, other = lax.optimization_barrier((doc_pieces, mine, other))
    (share, features), (target_share, _) = embed_docs.shape, embed_targets.shape
    n, m = share * cols, target_share * rows
    ratio = (n * rows) / (m * cols)
    product = 6 * n * m * features
    doc_vector, target_vector = ((n // LANES, LANES), f32), ((m // LANES, LANES), f32)
    doc_parts, target_parts = ((cols, *doc_vector[0]), f32), ((rows, *target_vector[0]), f32)
    docs, targets, tile, target_zero, part = run(
        kernel_tile,
        (start.reshape(target_vector[0]), *doc_pieces, *mine, *other),
        [((n, features), f32), ((m, features), f32), ((n, m), f32), target_vector, doc_parts],
        [((n, 3 * features), bf16), ((m, 3 * features), bf16)],
        limit=28, kept=(2,), flops=product, place=place,
    )

    def step(kernel, part, axis, *extra, over_docs):
        outs = [doc_vector, target_parts] if over_docs else [target_vector, doc_parts]
        return run(kernel, (tile, swap(part, axis), *extra), outs, held=HELD, flops=2 * n * m)

    doc_one, part = step(kernel_doc_one, part, COL, over_docs=True)
    target_one, part = step(kernel_target, part, ROW, over_docs=False)
    doc_two, part = step(kernel_doc_two, part, COL, over_docs=True)
    target_two, part = step(kernel_target, part, ROW, over_docs=False)
    bar_two, part = step(partial(kernel_bar_two, ratio), part, COL, doc_two, over_docs=True)
    bar_one, part = step(kernel_bar_one, part, ROW, target_one, over_docs=False)
    top, low, mass, *doc_pieces = run(
        partial(kernel_docs, ratio),
        (tile, swap(part, COL), doc_one, doc_two, bar_two, target_zero, target_one, target_two, bar_one, targets),
        [((n, m), bf16), ((n, m), bf16), target_vector] + [((n // SIZES["y"], features), f32)] * SIZES["y"],
        [((4, n, LANES), f32), ((m, 2 * features), bf16), ((n, features), f32)],
        limit=32, held=HELD, kept=(0, 1), flops=product, place=place,
    )
    doc_pieces = ring(doc_pieces, "y")
    other, mine = run(
        kernel_targets, (top, low, mass, docs, targets), [((m // 2, features), f32)] * 2, [((2 * features, n), bf16)],
        limit=24, held=(0, 1), flops=product, place=place,
    )
    (mine,) = run(kernel_pair, (mine, other_core(other)), [((m // 2, features), f32)])
    doc_pieces = run(kernel_pieces, doc_pieces, [((share, features), f32)] * SIZES["z_hi"], place=place)
    doc_pieces = ring(doc_pieces, "z_hi")
    blocks = swap(mine.reshape(rows // 2, target_share, features), ("z_lo", "x"))
    grads = run(
        kernel_grads, (embed_docs, *doc_pieces, blocks), [((share, features), f32), ((target_share, features), f32)]
    )
    return lax.while_loop(
        lambda state: state[0],
        lambda state: (False, *log_domain(embed_docs, embed_targets, start)),
        (jnp.isnan(jnp.sum(bar_two)), *grads),
    )[1:]


def solution(mesh):
    axes = ROW + COL
    fine = jax.sharding.Mesh(mesh.devices.reshape([SIZES[a] for a in axes]), axes)
    return jax.shard_map(
        local,
        mesh=fine,
        in_specs=(P(ROW + COL, None), P(COL + ROW, None), P(COL)),
        out_specs=(P(ROW + COL, None), P(COL + ROW, None)),
        check_vma=False,
    )
```

```python
import math
from functools import partial

import jax
import jax.numpy as jnp
from jax import lax
from jax.experimental import pallas as pl
from jax.experimental.pallas import tpu as pltpu
from jax.sharding import PartitionSpec as P

smoothing_epsilon = 0.05
EXPONENT_MAX = 40.0
LOW, HIGH = 1e-25, 1e25
FIRST_LOW = 1e-9
KEPT, HELD = (0,), (0,)
ROW, COL = ("z_lo", "x", "core"), ("y", "z_hi")
SIZES = {"z_lo": 2, "x": 4, "core": 2, "y": 4, "z_hi": 4}


def row_log_mass(scores):
    largest = lax.pmax(jnp.max(scores, axis=1), COL)
    mass_all = lax.psum(jnp.sum(jnp.exp(scores - largest[:, None]), axis=1), COL)
    return largest + jnp.log(mass_all)


def column_log_mass(scores):
    largest = lax.pmax(jnp.max(scores, axis=0), ROW)
    mass_all = lax.psum(jnp.sum(jnp.exp(scores - largest[None, :]), axis=0), ROW)
    return largest + jnp.log(mass_all)


def log_domain(embed_docs, embed_targets, start):
    doc_block, target_block = gather(embed_docs, COL), gather(embed_targets, ROW)
    highest = lax.Precision.HIGHEST
    distance_tile = (
        jnp.sum(doc_block * doc_block, axis=1)[:, None]
        + jnp.sum(target_block * target_block, axis=1)[None, :]
        - 2.0 * jnp.dot(doc_block, target_block.T, precision=highest)
    )
    texts = distance_tile.shape[0] * lax.axis_size(ROW)
    goals = distance_tile.shape[1] * lax.axis_size(COL)
    ratio = texts / goals
    t = smoothing_epsilon
    row_log_one = row_log_mass((start[None, :] - distance_tile) / t)
    doc_one = t * math.log(goals) - t * row_log_one
    col_log_one = column_log_mass((doc_one[:, None] - distance_tile) / t)
    target_one = t * math.log(texts) - t * col_log_one
    row_log_two = row_log_mass((target_one[None, :] - distance_tile) / t)
    doc_two = t * math.log(goals) - t * row_log_two
    col_log_two = column_log_mass((doc_two[:, None] - distance_tile) / t)
    plan = jnp.exp((doc_two[:, None] - distance_tile) / t - col_log_two[None, :])
    adjoint = ratio * plan
    doc_bar_two = 1.0 - ratio * lax.psum(jnp.sum(plan, axis=1), COL)
    plan = jnp.exp((target_one[None, :] - distance_tile) / t - row_log_two[:, None])
    weighted = doc_bar_two[:, None] * plan
    adjoint = adjoint + weighted
    target_bar_one = -lax.psum(jnp.sum(weighted, axis=0), ROW)
    plan = jnp.exp((doc_one[:, None] - distance_tile) / t - col_log_one[None, :])
    weighted = target_bar_one[None, :] * plan
    adjoint = adjoint + weighted
    doc_bar_one = -lax.psum(jnp.sum(weighted, axis=1), COL)
    plan = jnp.exp((start[None, :] - distance_tile) / t - row_log_one[:, None])
    adjoint = adjoint + doc_bar_one[:, None] * plan
    doc_part = 2.0 * (
        jnp.sum(adjoint, axis=1)[:, None] * doc_block
        - jnp.dot(adjoint, target_block, precision=highest)
    )
    crossed = lax.dot_general(adjoint, doc_block, (((0,), (0,)), ((), ())), precision=highest)
    target_part = 2.0 * (jnp.sum(adjoint, axis=0)[:, None] * target_block - crossed)
    return scatter(doc_part, COL), scatter(target_part, ROW)


LANES = 128
f32, bf16 = jnp.float32, jnp.bfloat16


def swap(blocks, axis):
    return lax.all_to_all(blocks, axis, 0, 0)


def gather(block, axis):
    devices = lax.axis_size(axis)
    pieces = swap(jnp.broadcast_to(block[None], (devices, *block.shape)), axis)
    return pieces.reshape(devices * block.shape[0], *block.shape[1:])


def scatter(block, axis):
    devices = lax.axis_size(axis)
    pieces = block.reshape(devices, block.shape[0] // devices, *block.shape[1:])
    return jnp.sum(swap(pieces, axis), axis=0)


def inverse(mass, low, high):
    return jnp.where((mass >= low) & (mass <= high), 1.0 / mass, jnp.nan)


def halves(values):
    top = values.astype(bf16)
    return top, (values - top.astype(f32)).astype(bf16)


def spans(size, step):
    return [slice(i, i + step) for i in range(0, size, step)]


def upright(vector):
    return jnp.transpose(jnp.broadcast_to(vector, (LANES, LANES)))


def lane_total(block):
    return jnp.sum(jnp.transpose(block), axis=0, keepdims=True)


def row_sums(tile, weight):
    out = []
    for rows in spans(tile.shape[0], LANES):
        acc = None
        for c, cols in enumerate(spans(tile.shape[1], LANES)):
            term = tile[rows, cols] * weight[c : c + 1, :]
            acc = term if acc is None else acc + term
        out.append(lane_total(acc))
    return jnp.concatenate(out, axis=0)


def column_sums(tile, weight):
    columns = spans(tile.shape[1], LANES)
    acc = [None] * len(columns)
    for r, rows in enumerate(spans(tile.shape[0], LANES)):
        factor = upright(weight[r : r + 1, :])
        for c, cols in enumerate(columns):
            term = jnp.sum((tile[rows, cols] * factor).reshape(-1, 8, LANES), axis=0)
            acc[c] = term if acc[c] is None else acc[c] + term
    return jnp.concatenate([jnp.sum(a, axis=0, keepdims=True) for a in acc], axis=0)


def spread(ref, values):
    ref[...] = jnp.broadcast_to(values[None], ref.shape)


def turned(place, by, size):
    return lax.rem(place + by, size)


def kernel_tile(place, start, *refs):
    (ys, zs), (xs, ls) = (SIZES["y"], SIZES["z_hi"]), (SIZES["x"], SIZES["z_lo"])
    doc_pieces, mine, other = refs[:ys], refs[ys : ys + xs], refs[ys + xs : ys + 2 * xs]
    docs, targets, tile, weight_out, part, doc_wide, target_wide = refs[ys + 2 * xs :]
    features = docs.shape[1]
    share, target_share = docs.shape[0] // (ys * zs), targets.shape[0] // (2 * xs * ls)
    for k, source in enumerate(doc_pieces):
        for j in range(zs):
            at = (turned(place[0], ys - k, ys) * zs + turned(place[1], zs - j, zs)) * share
            docs[pl.ds(pl.multiple_of(at, share), share), :] = source[j * share : (j + 1) * share, :]
    for core, pieces in ((place[2], mine), (1 - place[2], other)):
        for k, source in enumerate(pieces):
            for j in range(ls):
                at = ((core * ls + turned(place[4], ls - j, ls)) * xs + turned(place[3], xs - k, xs)) * target_share
                targets[pl.ds(pl.multiple_of(at, target_share), target_share), :] = source[
                    j * target_share : (j + 1) * target_share, :
                ]
    for source, wide, order in ((docs, doc_wide, (0, 0, 1)), (targets, target_wide, (0, 1, 0))):
        for rows in spans(source.shape[0], 256):
            pair = halves(source[rows, :])
            for k, which in enumerate(order):
                wide[rows, k * features : (k + 1) * features] = pair[which]
    norms = []
    for rows in spans(targets.shape[0], LANES):
        squares = targets[rows, :] * targets[rows, :]
        norms.append(lane_total(sum(squares[:, cols] for cols in spans(features, LANES))))
    count = start.shape[0]
    begin = jnp.concatenate([start[i : i + 1, :] for c in range(2) for i in range(c, count, 2)], axis=0)
    weight = jnp.exp((begin - jnp.concatenate(norms, axis=0)) / smoothing_epsilon)
    largest = None
    for c, cols in enumerate(spans(targets.shape[0], 256)):
        dots = lax.dot_general(
            doc_wide[...], target_wide[cols, :], (((1,), (1,)), ((), ())), preferred_element_type=f32
        )
        dots = dots * (2.0 / smoothing_epsilon)
        masses = jnp.exp(dots)
        tile[:, cols] = masses
        peak = jnp.max(jnp.abs(dots).reshape(-1, 8, 256), axis=0)
        largest = peak if largest is None else jnp.maximum(largest, peak)
    fits = jnp.max(largest) <= EXPONENT_MAX
    weight = jnp.where(fits, weight, jnp.nan)
    weight_out[...] = weight
    spread(part, row_sums(tile, weight))


def kernel_doc_one(tile, parts, weight_out, part):
    weight = inverse(jnp.sum(parts[...], axis=0), FIRST_LOW, HIGH)
    weight_out[...] = weight
    spread(part, column_sums(tile, weight))


def kernel_doc_two(tile, parts, weight_out, part):
    weight = inverse(jnp.sum(parts[...], axis=0), LOW, HIGH)
    weight_out[...] = weight
    spread(part, column_sums(tile, weight))


def kernel_target(tile, parts, weight_out, part):
    weight = inverse(jnp.sum(parts[...], axis=0), LOW, HIGH)
    weight_out[...] = weight
    spread(part, row_sums(tile, weight))


def kernel_bar_two(ratio, tile, parts, doc_two, weight_out, part):
    scale = doc_two[...]
    weight = scale * (1.0 - ratio * scale * jnp.sum(parts[...], axis=0))
    weight_out[...] = weight
    spread(part, column_sums(tile, weight))


def kernel_bar_one(tile, parts, target_one, weight_out, part):
    scale = target_one[...]
    weight = -scale * scale * jnp.sum(parts[...], axis=0)
    weight_out[...] = weight
    spread(part, row_sums(tile, weight))


def kernel_docs(ratio, place, tile, parts, doc_one, doc_two, bar_two, target_zero, target_one, target_two, bar_one,
                targets, top, low, mass, *refs):
    pieces, (factors, wide, sums) = refs[:-3], refs[-3:]
    features = targets.shape[1]
    for rows in spans(targets.shape[0], 256):
        pair = halves(targets[rows, :])
        wide[rows, :features], wide[rows, features:] = pair
    one = doc_one[...]
    bar_zero = -one * one * jnp.sum(parts[...], axis=0)
    by_row = (bar_zero, ratio * doc_two[...], bar_two[...], one)
    by_column = (target_zero[...], target_two[...], target_one[...], bar_one[...])
    columns = spans(tile.shape[1], LANES)
    acc = [None] * len(columns)
    for r, rows in enumerate(spans(tile.shape[0], LANES)):
        for k, values in enumerate(by_row):
            factors[k, rows, :] = upright(values[r : r + 1, :])

    def form(rows):
        a = [factors[i, rows, :] for i in range(4)]
        for c, cols in enumerate(columns):
            b = [v[c : c + 1, :] for v in by_column]
            adjoint = tile[rows, cols] * ((a[0] * b[0] + a[1] * b[1]) + (a[2] * b[2] + a[3] * b[3]))
            term = jnp.sum(adjoint.reshape(-1, 8, LANES), axis=0)
            acc[c] = term if acc[c] is None else acc[c] + term
            top[rows, cols], low[rows, cols] = halves(adjoint)

    def multiply(block):
        both = jnp.dot(top[block, :], wide[...], preferred_element_type=f32)
        rest = jnp.dot(low[block, :], wide[:, :features], preferred_element_type=f32)
        sums[block, :] = (both[:, :features] + both[:, features:]) + rest

    size = pieces[0].shape[0]
    for block in spans(tile.shape[0], 256):
        for rows in spans(256, 32):
            form(slice(block.start + rows.start, block.start + rows.stop))
        multiply(block)
    for k, piece in enumerate(pieces):
        piece[...] = sums[pl.ds(pl.multiple_of(turned(place[0], k, len(pieces)) * size, size), size), :]
    mass[...] = jnp.concatenate([jnp.sum(a, axis=0, keepdims=True) for a in acc], axis=0)


def kernel_targets(place, top, low, mass, docs, targets, other, mine, flat):
    features = docs.shape[1]
    for rows in spans(docs.shape[0], 256):
        pair = halves(jnp.transpose(docs[rows, :]))
        flat[:features, rows], flat[features:, rows] = pair
    half = mine.shape[0]
    for core, out in ((1 - place[2], other), (place[2], mine)):
        for inner in spans(half, 256):
            first = pl.multiple_of(core * half + inner.start, 256)
            cols = pl.ds(first, 256)
            both = jnp.dot(flat[...], top[:, cols], preferred_element_type=f32)
            rest = jnp.dot(flat[:features, :], low[:, cols], preferred_element_type=f32)
            crossed = jnp.transpose((both[:features] + both[features:]) + rest)
            for rows in spans(256, LANES):
                at = core * (half // LANES) + (inner.start + rows.start) // LANES
                weight = upright(mass[pl.ds(at, 1), :])
                here = pl.ds(first + rows.start, LANES)
                for part in spans(features, LANES):
                    out[inner.start + rows.start : inner.start + rows.stop, part] = 2.0 * (
                        weight * targets[here, part] - crossed[rows, part]
                    )


def kernel_pieces(place, *refs):
    parts, pieces = refs[: SIZES["y"]], refs[SIZES["y"] :]
    size = pieces[0].shape[0]
    for k, piece in enumerate(pieces):
        rows = pl.ds(pl.multiple_of(turned(place[1], k, len(pieces)) * size, size), size)
        piece[...] = sum(part[rows, :] for part in parts)


def kernel_pair(one, two, out):
    out[...] = one[...] + two[...]


def kernel_grads(own, *refs):
    parts, (blocks, grad_docs, grad_targets) = refs[:-3], refs[-3:]
    grad_docs[...] = 2.0 * (own[...] - sum(part[...] for part in parts))
    grad_targets[...] = jnp.sum(blocks[...], axis=0)


def run(kernel, args, outs, scratch=(), limit=16, held=(), kept=(), flops=0, place=None):
    args = [pltpu.with_memory_space_constraint(a, pltpu.VMEM) if i in held else a for i, a in enumerate(args)]
    shapes = [pltpu.VMEM(*o) if i in kept else jax.ShapeDtypeStruct(*o) for i, o in enumerate(outs)]
    whole = pl.BlockSpec(memory_space=pltpu.VMEM)
    specs = [whole] * len(args)
    if place is not None:
        args, specs = [place, *args], [pl.BlockSpec(memory_space=pltpu.SMEM), *specs]
    size = sum(math.prod(a.shape) * a.dtype.itemsize for a in args)
    return pl.pallas_call(
        kernel,
        out_shape=shapes,
        in_specs=specs,
        out_specs=[whole] * len(outs),
        scratch_shapes=[pltpu.VMEM(*s) for s in scratch],
        compiler_params=pltpu.CompilerParams(vmem_limit_bytes=limit << 20),
        cost_estimate=pl.CostEstimate(flops=flops, bytes_accessed=size, transcendentals=0),
    )(*args)


def ring(blocks, axis):
    size = SIZES[axis]
    out = [blocks[0]] * size
    for k in sorted(range(1, size), key=lambda k: (min(k, size - k), k)):
        out[k] = lax.ppermute(blocks[k], axis, [(i, (i + k) % size) for i in range(size)])
    return out


def other_core(block):
    return lax.ppermute(block, "core", [(0, 1), (1, 0)])


def local(embed_docs, embed_targets, start):
    rows, cols = lax.axis_size(ROW), lax.axis_size(COL)
    place = jnp.stack([lax.axis_index(a) for a in ("y", "z_hi", "core", "x", "z_lo")]).astype(jnp.int32)
    near, beside = ring([embed_docs] * SIZES["z_hi"], "z_hi"), ring([embed_targets] * SIZES["z_lo"], "z_lo")
    mine = ring([jnp.concatenate(beside, axis=0)] * SIZES["x"], "x")
    doc_pieces = ring([jnp.concatenate(near, axis=0)] * SIZES["y"], "y")
    other = [other_core(block) for block in mine]
    doc_pieces, mine, other = lax.optimization_barrier((doc_pieces, mine, other))
    (share, features), (target_share, _) = embed_docs.shape, embed_targets.shape
    n, m = share * cols, target_share * rows
    ratio = (n * rows) / (m * cols)
    product = 6 * n * m * features
    doc_vector, target_vector = ((n // LANES, LANES), f32), ((m // LANES, LANES), f32)
    doc_parts, target_parts = ((cols, *doc_vector[0]), f32), ((rows, *target_vector[0]), f32)
    docs, targets, tile, target_zero, part = run(
        kernel_tile,
        (start.reshape(target_vector[0]), *doc_pieces, *mine, *other),
        [((n, features), f32), ((m, features), f32), ((n, m), f32), target_vector, doc_parts],
        [((n, 3 * features), bf16), ((m, 3 * features), bf16)],
        limit=28, kept=(2,), flops=product, place=place,
    )

    def step(kernel, part, axis, *extra, over_docs):
        outs = [doc_vector, target_parts] if over_docs else [target_vector, doc_parts]
        return run(kernel, (tile, swap(part, axis), *extra), outs, held=HELD, flops=2 * n * m)

    doc_one, part = step(kernel_doc_one, part, COL, over_docs=True)
    target_one, part = step(kernel_target, part, ROW, over_docs=False)
    doc_two, part = step(kernel_doc_two, part, COL, over_docs=True)
    target_two, part = step(kernel_target, part, ROW, over_docs=False)
    bar_two, part = step(partial(kernel_bar_two, ratio), part, COL, doc_two, over_docs=True)
    bar_one, part = step(kernel_bar_one, part, ROW, target_one, over_docs=False)
    top, low, mass, *doc_pieces = run(
        partial(kernel_docs, ratio),
        (tile, swap(part, COL), doc_one, doc_two, bar_two, target_zero, target_one, target_two, bar_one, targets),
        [((n, m), bf16), ((n, m), bf16), target_vector] + [((n // SIZES["y"], features), f32)] * SIZES["y"],
        [((4, n, LANES), f32), ((m, 2 * features), bf16), ((n, features), f32)],
        limit=32, held=HELD, kept=(0, 1), flops=product, place=place,
    )
    doc_pieces = ring(doc_pieces, "y")
    other, mine = run(
        kernel_targets, (top, low, mass, docs, targets), [((m // 2, features), f32)] * 2, [((2 * features, n), bf16)],
        limit=24, held=(0, 1), flops=product, place=place,
    )
    (mine,) = run(kernel_pair, (mine, other_core(other)), [((m // 2, features), f32)])
    doc_pieces = run(kernel_pieces, doc_pieces, [((share, features), f32)] * SIZES["z_hi"], place=place)
    doc_pieces = ring(doc_pieces, "z_hi")
    blocks = swap(mine.reshape(rows // 2, target_share, features), ("z_lo", "x"))
    grads = run(
        kernel_grads, (embed_docs, *doc_pieces, blocks), [((share, features), f32), ((target_share, features), f32)]
    )
    return lax.while_loop(
        lambda state: state[0],
        lambda state: (False, *log_domain(embed_docs, embed_targets, start)),
        (jnp.isnan(jnp.sum(bar_two)), *grads),
    )[1:]


def solution(mesh):
    axes = ROW + COL
    fine = jax.sharding.Mesh(mesh.devices.reshape([SIZES[a] for a in axes]), axes)
    return jax.shard_map(
        local,
        mesh=fine,
        in_specs=(P(ROW + COL, None), P(COL + ROW, None), P(COL)),
        out_specs=(P(ROW + COL, None), P(COL + ROW, None)),
        check_vma=False,
    )
```
